512 devices in a mesh: lag: 16 (over y, x_hi, core), row: 32 (over z, x_lo).
Axes of the slice: x: 4 (x_hi: 2, x_lo: 2; x = x_hi * 2 + x_lo), y: 4, z: 16, core: 2. Of those that a mesh axis runs over, the one named last changes fastest.
Arguments:
- lag_ops: float32 [32, 3072, 3072], P('lag', 'row'), may hold values from -0.109375 to 0.109375
- inverse: float32 [3072, 3072], P('row'), may hold values from -0.109375 to 0.109375
- history: float32 [32, 3072, 128], P('lag', 'row'), may hold values from -6 to 6
- loads: float32 [3, 3072, 128], P(None, 'row'), may hold values from -6 to 6
Outputs:
- current: float32 [3072, 128], P('row')
- future: float32 [32, 3072, 128], P('lag', 'row')
The draws below stay inside these ranges and needn't reach their ends.
All inputs are finite; a program needn't handle non-finite values.
Results may differ from the reference program's by a relative error of at most 0.00011.
Values sent between devices are 32-bit elements; how exact they have to be, the bound alone decides.
A program may use at most 64 MiB of HBM per device.

```python
import jax
import jax.numpy as jnp
from jax import lax

U = 3072
LOADS = 128
STEPS = 3
LAGS = 32


def block_levels(stream_key, dims, cuts, least, high):
    def one(dim, shards_of):
        draws = jax.random.uniform(jax.random.fold_in(jax.random.fold_in(stream_key, 6), dim), (shards_of,), jnp.float32, least / len(cuts), high / len(cuts))
        return jnp.repeat(jnp.exp(draws), dims[dim] // shards_of).reshape((-1,) + (1,) * (len(dims) - dim - 1))

    level = one(*cuts[0])
    for cut in cuts[1:]:
        level = level * one(*cut)
    return level


def normal_values(stream_key, dims, scale, reach, cuts=(), held_as=jnp.bfloat16):
    values = jax.random.normal(stream_key, dims, jnp.float32) * scale
    if len(cuts) > 0:
        values = block_levels(stream_key, dims, cuts, -0.22, 0.18) * values
    return jnp.clip(values, min=-reach, max=reach).astype(held_as)


def setup_inputs(seed: int = 0) -> dict:
    arg_keys = jax.random.split(jax.random.key(seed), 5)
    return {
        "lag_ops": normal_values(arg_keys[0], (LAGS, U, U), U ** -0.5, 0.109375, ((0, 16), (1, 32)), jnp.float32),
        "inverse": normal_values(arg_keys[1], (U, U), U ** -0.5, 0.109375, ((0, 32),), jnp.float32),
        "history": normal_values(arg_keys[2], (LAGS, U, LOADS), 1.0, 6.0, ((0, 16), (1, 32)), jnp.float32),
        "loads": normal_values(arg_keys[3], (STEPS, U, LOADS), 1.0, 6.0, ((1, 32),), jnp.float32),
    }


def reference(lag_ops, inverse, history, loads):
    acc = history
    current = jnp.zeros((U, LOADS), jnp.float32)
    for step in range(STEPS):
        rhs = loads[step] - acc[0]
        current = jnp.dot(inverse, rhs, precision=lax.Precision.HIGHEST, preferred_element_type=jnp.float32)
        product = jnp.einsum("kuv,vb->kub", lag_ops, current, precision=lax.Precision.HIGHEST)
        shifted = jnp.concatenate([acc[1:], jnp.zeros((1, U, LOADS), jnp.float32)], axis=0)
        acc = shifted + product
    return current, acc
```

```python
import functools

import jax
import jax.numpy as jnp
from jax import lax
from jax.experimental import pallas as pl
from jax.experimental.pallas import tpu as pltpu
from jax.sharding import PartitionSpec as P

MESH = pl.DeviceIdType.MESH
F32 = jnp.float32
BF16 = jnp.bfloat16
NG = 16
NP = 8
NZ = 16
RB = 96
U = 3072
PC = U // NP
HR = RB // 2


def split(x):
    hi = x.astype(BF16).astype(F32)
    return hi, x - hi


def kernel(
    lag_h, inv_h, hist_h, loads_h, cur_ref, fut_ref,
    lagv, invv, hist, loads, lb, wv, w0, w1, wl, xr, xf, tbuf, rbuf, inc, accs, pa,
    lsem, gs, gr, rss, rsr, lss, lsr, las, lar, lbs, lbr, pgs, pgr, sgs, sgr, shs, shr,
):
    g = lax.axis_index("lag")
    r = lax.axis_index("row")
    z, xl = r // 2, r % 2
    p, c = g // 2, g % 2
    xh = p % 2

    def rc(src, dst, ss, rs, gg, rr):
        return pltpu.make_async_remote_copy(
            src_ref=src, dst_ref=dst, send_sem=ss, recv_sem=rs, device_id=(gg, rr), device_id_type=MESH
        )

    def loop(n, f):
        lax.fori_loop(0, n, lambda i, _: (f(i), 0)[1], 0)

    barrier = pltpu.get_barrier_semaphore()

    def greet(gg, rr):
        pl.semaphore_signal(barrier, inc=1, device_id=(gg, rr), device_id_type=MESH)

    loop(2 * NZ - 1, lambda i: greet(g, (r + 1 + i) % (2 * NZ)))
    loop(NG - 1, lambda i: greet((g + 1 + i) % NG, r))
    loop(4, lambda i: greet(i * 4 + (1 - xh) * 2 + c, z * 2 + 1 - xl))

    loc = [
        pltpu.make_async_copy(inv_h, invv, lsem.at[0]),
        pltpu.make_async_copy(lag_h, lagv, lsem.at[1]),
        pltpu.make_async_copy(hist_h, hist, lsem.at[2]),
        pltpu.make_async_copy(loads_h, loads, lsem.at[3]),
    ]
    for cp in (loc[3], loc[2], loc[0], loc[1]):
        cp.start()
    root = pltpu.make_async_copy(lag_h, lb, lsem.at[4])

    @pl.when(g == 0)
    def _():
        root.start()

    loc[3].wait()
    loc[2].wait()

    def turned(n, h):
        d = loads[n] - hist[h]
        return jnp.concatenate([d, jnp.zeros((128 - RB, 128), F32)], axis=0).T.reshape(NG, 8, 128)

    @pl.when(g == 0)
    def _():
        t0 = turned(0, 0)
        tbuf[0] = t0
        rbuf[0] = t0[0]
        t1 = turned(1, 1)
        tbuf[1] = t1
        rbuf[1] = t1[0]
        root.wait()

    @pl.when(g == 1)
    def _():
        t2 = turned(2, 0)
        tbuf[2] = t2
        rbuf[2] = t2[1]

    pl.semaphore_wait(barrier, 2 * NZ - 1 + NG - 1 + 4)

    def rscatter(n, gg):
        return rc(tbuf.at[n, gg], rbuf.at[n], rss.at[n, gg], rsr.at[n], gg, r)

    def piece(n, cc, pp):
        return lb.at[n, pl.ds(pl.multiple_of(cc * HR, 8), HR), pl.ds(pl.multiple_of(pp * PC, 128), PC)]

    def lscatter(n, gg):
        v = piece(n, gg % 2, gg // 2)
        return rc(v, v, lss.at[n, gg], lsr.at[n], gg, r)

    @pl.when(g == 0)
    def _():
        loop(NG - 1, lambda i: rscatter(0, NG - 1 - i).start())
        loop(NG - 1, lambda i: lscatter(0, NG - 1 - i).start())
        loop(NG - 1, lambda i: rscatter(1, NG - 1 - i).start())
        loop(NG - 1, lambda i: lscatter(1, NG - 1 - i).start())

    @pl.when(g == 1)
    def _():
        loop(NG - 1, lambda i: rscatter(2, (g + 1 + i) % NG).start())

    def shift(n, src):
        return rc(src, inc.at[n], shs.at[n], shr.at[n], g - 1, r)

    @pl.when(g > 0)
    def _():
        shift(0, hist.at[0]).start()

    def prep(src, dst):
        dst[...] = jnp.zeros_like(dst)

        def some(i):
            blk = src[:, pl.ds(pl.multiple_of(i * 384, 128), 384)]
            for j in range(4):
                hi, lo = split(blk[:, j * RB : (j + 1) * RB])
                lanes = slice((j % 2) * 128, (j % 2) * 128 + RB)
                dst[2 * i + j // 2, 0:RB, lanes] = hi.astype(BF16)
                dst[2 * i + j // 2, 128 : 128 + RB, lanes] = lo.astype(BF16)

        loop(8, some)

    def prep_lags():
        wl[...] = jnp.zeros_like(wl)

        def some(i):
            for a in range(2):
                blk = lagv[a, :, pl.ds(pl.multiple_of(i * 384, 128), 384)]
                for j in range(4):
                    hi, lo = split(blk[:, j * RB : (j + 1) * RB])
                    wl[i, a * RB : (a + 1) * RB, j * 128 : j * 128 + RB] = hi.astype(BF16)
                    wl[i, (2 + a) * RB : (3 + a) * RB, j * 128 : j * 128 + RB] = lo.astype(BF16)

        loop(8, some)

    def at_turn(k):
        return (z + (2 * (k % 2) - 1) * (8 - (k + 1) // 2) + NZ) % NZ

    def block_to(xb, par, k, f):
        zz = at_turn(k)
        xx = (xl + 1 - f) % 2
        return rc(xb.at[z, xl], xb.at[z, xl], gs.at[par, 2 * k + f], gr.at[par, r], g, zz * 2 + xx)

    def block_from(xb, par, zz, xx):
        v = xb.at[zz, xx]
        return rc(v, v, gs.at[par, 0], gr.at[par, zz * 2 + xx], g, r)

    def send(xb, par, block):
        xb[z, xl] = block

        def one(i):
            block_to(xb, par, i // 2, i % 2).start()

        loop(2 * NZ - 1, one)

    def sent(xb, par):
        loop(2 * NZ - 1, lambda i: block_to(xb, par, i // 2, i % 2).wait_send())

    def product(xb, w, par=None):
        def one(i, acc):
            k = NZ - 1 - i
            zz = at_turn(k)
            if par is not None:
                block_from(xb, par, zz, 1 - xl).wait_recv()

                @pl.when(i > 0)
                def _():
                    block_from(xb, par, zz, xl).wait_recv()

            x = jnp.concatenate([xb[zz, 0], xb[zz, 1]], axis=1)
            hi, lo = split(x)
            lhs = jnp.concatenate([hi, lo], axis=0).astype(BF16)
            return acc + lax.dot_general(lhs, w[zz], (((1,), (1,)), ((), ())), preferred_element_type=F32)

        acc = lax.fori_loop(0, NZ, one, jnp.zeros((16, 256), F32))
        return (acc[0:8, 0:128] + acc[8:16, 0:128]) + (acc[0:8, 128:256] + acc[8:16, 128:256])

    def lgather(n, pp):
        v = piece(n, c, p)
        return rc(v, v, las.at[n, pp], lar.at[n, p], pp * 2 + c, r)

    def lgathered(n, pp):
        v = piece(n, c, pp)
        return rc(v, v, las.at[n, 0], lar.at[n, pp], g, r)

    def half(n, cc):
        return lb.at[n, pl.ds(pl.multiple_of(cc * HR, 8), HR), :]

    def lsib(n):
        return rc(half(n, c), half(n, c), lbs.at[n], lbr.at[n], g + 1 - 2 * c, r)

    def relay(n):
        @pl.when(g > 0)
        def _():
            lscatter(n, g).wait_recv()

        def one(i):
            pp = (p + 1 + i) % NP

            @pl.when(pp * 2 + c > 0)
            def _():
                lgather(n, pp).start()

        loop(NP - 1, one)

    def assemble(n):
        @pl.when(g > 0)
        def _():
            loop(NP - 1, lambda i: lgathered(n, (p + 1 + i) % NP).wait_recv())

        @pl.when(g != 1)
        def _():
            lsib(n).start()

        @pl.when(g > 0)
        def _():
            rc(half(n, 1 - c), half(n, 1 - c), lbs.at[n], lbr.at[n], g, r).wait_recv()

    def plane(n, pp):
        xx = (xl + (pp % 2 + xh) % 2) % 2
        return rc(xf.at[n, g], xf.at[n, g], pgs.at[n, pp], pgr.at[n, p], pp * 2 + c, z * 2 + xx)

    def planed(n, pp):
        v = xf.at[n, pp * 2 + c]
        return rc(v, v, pgs.at[n, 0], pgr.at[n, pp], g, r)

    def sib(n, pp):
        v = xf.at[n, pp * 2 + c]
        return rc(v, v, sgs.at[n, pp], sgr.at[n, pp], g + 1 - 2 * c, r)

    def sibbed(n, pp):
        v = xf.at[n, pp * 2 + 1 - c]
        return rc(v, v, sgs.at[n, 0], sgr.at[n, pp], g, r)

    def spread(n):
        sib(n, p).start()
        loop(NP - 1, lambda i: plane(n, (p + NP - 1 - i) % NP).start())

    def forward(n):
        def one(i):
            pp = (p + 1 + i) % NP
            planed(n, pp).wait_recv()
            sib(n, pp).start()

        loop(NP - 1, one)

    def lag_product(n):
        loop(NP, lambda i: sibbed(n, i).wait_recv())
        pa[...] = jnp.zeros_like(pa)

        def one(i):
            x = jnp.concatenate(
                [xf[n, :, 2 * i + j // 2, j % 2].reshape(128, 128) for j in range(4)], axis=1
            )
            hi, lo = split(x)
            rhs = jnp.concatenate([hi, lo], axis=0).astype(BF16)
            pa[...] += lax.dot_general(wl[i], rhs, (((1,), (1,)), ((), ())), preferred_element_type=F32)

        loop(8, one)

    def lag_rows(a):
        lo, hi = a * RB, (a + 1) * RB
        big = pa[lo:hi, 0:128] + pa[lo:hi, 128:256]
        small = pa[2 * RB + lo : 2 * RB + hi, 0:128] + pa[2 * RB + lo : 2 * RB + hi, 128:256]
        return big + small

    def incoming(n):
        @pl.when(g < NG - 1)
        def _():
            rc(inc.at[n], inc.at[n], shs.at[n], shr.at[n], g, r).wait_recv()

        @pl.when(g == NG - 1)
        def _():
            inc[n] = jnp.zeros((RB, 128), F32)

    def advance(n):
        lag_product(n)
        incoming(n)
        first = hist[1] if n == 0 else accs[n - 1, 1]
        accs[n, 0] = first + lag_rows(0)
        accs[n, 1] = inc[n] + lag_rows(1)

        @pl.when(g > 0)
        def _():
            shift(n + 1, accs.at[n, 0]).start()

    loc[0].wait()
    prep(invv, wv)
    loc[1].wait()

    def rwait(n):
        @pl.when(g != n // 2)
        def _():
            rscatter(n, g).wait_recv()

    rwait(0)
    send(xr.at[0], 0, rbuf[0])
    relay(0)
    prep_lags()
    now = product(xr.at[0], wv, 0)
    send(xf.at[0, g], 1, now)
    sent(xr.at[0], 0)
    relay(1)
    assemble(0)
    prep(lb.at[0], w0)
    rwait(1)
    now = rbuf[1] - product(xf.at[0, g], w0, 1)
    send(xr.at[1], 0, now)
    spread(0)
    sent(xf.at[0, g], 1)
    assemble(1)
    prep(lb.at[1], w1)
    rwait(2)
    late = rbuf[2] - product(xf.at[0, g], w1)
    now = product(xr.at[1], wv, 0)
    send(xf.at[1, g], 1, now)
    sent(xr.at[1], 0)
    forward(0)
    now = late - product(xf.at[1, g], w0, 1)
    send(xr.at[2], 0, now)
    spread(1)
    sent(xf.at[1, g], 1)
    advance(0)
    now = product(xr.at[2], wv, 0)
    send(xf.at[2, g], 1, now)
    sent(xr.at[2], 0)
    forward(1)
    advance(1)

    def arrived(i):
        zz = at_turn(NZ - 1 - i)
        block_from(xf.at[2, g], 1, zz, 1 - xl).wait_recv()

        @pl.when(i > 0)
        def _():
            block_from(xf.at[2, g], 1, zz, xl).wait_recv()

    loop(NZ, arrived)
    spread(2)
    sent(xf.at[2, g], 1)
    forward(2)
    lag_product(2)
    incoming(2)
    fut_ref[0] = accs[1, 1] + lag_rows(0)
    fut_ref[1] = inc[2] + lag_rows(1)
    cur_ref[...] = xf[2, :, z, xl].reshape(128, 128).T[0:RB]

    @pl.when(g == 0)
    def _():
        for n in range(2):
            loop(NG - 1, lambda i, n=n: rscatter(n, 1 + i).wait_send())
            loop(NG - 1, lambda i, n=n: lscatter(n, 1 + i).wait_send())

    @pl.when(g == 1)
    def _():
        loop(NG - 1, lambda i: rscatter(2, (g + 1 + i) % NG).wait_send())

    for n in range(2):

        def lsent(i, n=n):
            pp = (p + 1 + i) % NP

            @pl.when(pp * 2 + c > 0)
            def _():
                lgather(n, pp).wait_send()

        loop(NP - 1, lsent)

        @pl.when(g != 1)
        def _(n=n):
            lsib(n).wait_send()

    for n in range(3):
        loop(NP - 1, lambda i, n=n: plane(n, (p + 1 + i) % NP).wait_send())
        loop(NP, lambda i, n=n: sib(n, i).wait_send())

        @pl.when(g > 0)
        def _(n=n):
            shift(n, accs.at[0, 0]).wait_send()


def body(lag_ops, inverse, history, loads):
    anyspec = pl.BlockSpec(memory_space=pl.ANY)
    vspec = pl.BlockSpec(memory_space=pltpu.VMEM)
    dma = pltpu.SemaphoreType.DMA
    scratch = [
        pltpu.VMEM((2, RB, U), F32),
        pltpu.VMEM((RB, U), F32),
        pltpu.VMEM((2, RB, 128), F32),
        pltpu.VMEM((3, RB, 128), F32),
        pltpu.VMEM((2, RB, U), F32),
        pltpu.VMEM((NZ, 256, 256), BF16),
        pltpu.VMEM((NZ, 256, 256), BF16),
        pltpu.VMEM((NZ, 256, 256), BF16),
        pltpu.VMEM((8, 4 * RB, 512), BF16),
        pltpu.VMEM((3, NZ, 2, 8, 128), F32),
        pltpu.VMEM((3, NG, NZ, 2, 8, 128), F32),
        pltpu.VMEM((3, NG, 8, 128), F32),
        pltpu.VMEM((3, 8, 128), F32),
        pltpu.VMEM((3, RB, 128), F32),
        pltpu.VMEM((2, 2, RB, 128), F32),
        pltpu.VMEM((4 * RB, 256), F32),
        dma((5,)),
        dma((2, 2 * NZ)),
        dma((2, 2 * NZ)),
        dma((3, NG)),
        dma((3,)),
        dma((2, NG)),
        dma((2,)),
        dma((2, NP)),
        dma((2, NP)),
        dma((2,)),
        dma((2,)),
        dma((3, NP)),
        dma((3, NP)),
        dma((3, NP)),
        dma((3, NP)),
        dma((3,)),
        dma((3,)),
    ]
    return pl.pallas_call(
        kernel,
        out_shape=(
            jax.ShapeDtypeStruct((RB, 128), F32),
            jax.ShapeDtypeStruct((2, RB, 128), F32),
        ),
        in_specs=[anyspec] * 4,
        out_specs=(vspec, vspec),
        scratch_shapes=scratch,
        compiler_params=pltpu.CompilerParams(
            collective_id=0, has_side_effects=True, vmem_limit_bytes=48 * 2**20
        ),
    )(lag_ops, inverse, history, loads)


def solution(mesh):
    placed = (P("lag", "row", None), P("row", None), P("lag", "row", None), P(None, "row", None))
    return jax.shard_map(
        body,
        mesh=mesh,
        in_specs=placed,
        out_specs=(P("row", None), P("lag", "row", None)),
        check_vma=False,
    )
```

```python
import functools

import jax
import jax.numpy as jnp
from jax import lax
from jax.experimental import pallas as pl
from jax.experimental.pallas import tpu as pltpu
from jax.sharding import PartitionSpec as P

MESH = pl.DeviceIdType.MESH
F32 = jnp.float32
BF16 = jnp.bfloat16
NG = 16
NP = 8
NZ = 16
RB = 96
U = 3072
PC = U // NP
HR = RB // 2


def split(x):
    hi = x.astype(BF16).astype(F32)
    return hi, x - hi


def kernel(
    lag_h, inv_h, hist_h, loads_h, cur_ref, fut_ref,
    lagv, invv, hist, loads, lb, wv, w0, w1, wl, xr, xf, xc, tbuf, rbuf, inc, accs, pa,
    lsem, gs, gr, rss, rsr, lss, lsr, las, lar, lbs, lbr, pgs, pgr, sgs, sgr, shs, shr, qps, qpr, qss, qsr,
):
    g = lax.axis_index("lag")
    r = lax.axis_index("row")
    z, xl = r // 2, r % 2
    p, c = g // 2, g % 2
    xh = p % 2
    rx = (xl + xh) % 2

    def rc(src, dst, ss, rs, gg, rr):
        return pltpu.make_async_remote_copy(
            src_ref=src, dst_ref=dst, send_sem=ss, recv_sem=rs, device_id=(gg, rr), device_id_type=MESH
        )

    def loop(n, f):
        lax.fori_loop(0, n, lambda i, _: (f(i), 0)[1], 0)

    def over(pp):
        return z * 2 + (xl + xh + pp) % 2

    barrier = pltpu.get_barrier_semaphore()

    def greet(gg, rr):
        pl.semaphore_signal(barrier, inc=1, device_id=(gg, rr), device_id_type=MESH)

    loop(2 * NZ - 1, lambda i: greet(g, (r + 1 + i) % (2 * NZ)))
    loop(NG - 1, lambda i: greet((g + 1 + i) % NG, over((g + 1 + i) % NG // 2)))

    @pl.when((g > 0) & ((g - 1) // 2 % 2 != xh))
    def _():
        greet(g - 1, r)

    @pl.when((g < NG - 1) & ((g + 1) // 2 % 2 != xh))
    def _():
        greet(g + 1, r)

    extra = jnp.where((g > 0) & (g % 2 == 0), 1, 0) + jnp.where((g < NG - 1) & (g % 2 == 1), 1, 0)

    loc = [
        pltpu.make_async_copy(inv_h, invv, lsem.at[0]),
        pltpu.make_async_copy(lag_h, lagv, lsem.at[1]),
        pltpu.make_async_copy(hist_h, hist, lsem.at[2]),
        pltpu.make_async_copy(loads_h, loads, lsem.at[3]),
    ]
    for cp in (loc[3], loc[2], loc[0], loc[1]):
        cp.start()
    root = pltpu.make_async_copy(lag_h, lb, lsem.at[4])

    @pl.when(g == 0)
    def _():
        root.start()

    loc[3].wait()
    loc[2].wait()

    def turned(n, h):
        d = loads[n] - hist[h]
        return jnp.concatenate([d, jnp.zeros((128 - RB, 128), F32)], axis=0).T.reshape(NG, 8, 128)

    @pl.when(g == 0)
    def _():
        t0 = turned(0, 0)
        tbuf[0] = t0
        rbuf[0] = t0[0]
        t1 = turned(1, 1)
        tbuf[1] = t1
        rbuf[1] = t1[0]
        root.wait()

    @pl.when(g == 1)
    def _():
        t2 = turned(2, 0)
        tbuf[2] = t2
        rbuf[2] = t2[1]

    pl.semaphore_wait(barrier, 2 * NZ - 1 + NG - 1 + extra)

    def rscatter(n, gg):
        return rc(tbuf.at[n, gg], rbuf.at[n], rss.at[n, gg], rsr.at[n], gg, over(gg // 2))

    def piece(n, cc, pp):
        return lb.at[n, pl.ds(pl.multiple_of(cc * HR, 8), HR), pl.ds(pl.multiple_of(pp * PC, 128), PC)]

    def lscatter(n, gg):
        v = piece(n, gg % 2, gg // 2)
        return rc(v, v, lss.at[n, gg], lsr.at[n], gg, over(gg // 2))

    @pl.when(g == 0)
    def _():
        loop(NG - 1, lambda i: rscatter(0, NG - 1 - i).start())
        loop(NG - 1, lambda i: lscatter(0, NG - 1 - i).start())
        loop(NG - 1, lambda i: rscatter(1, NG - 1 - i).start())

    @pl.when(g == 1)
    def _():
        loop(NG - 1, lambda i: rscatter(2, (g + 1 + i) % NG).start())

    def shift(n, src):
        return rc(src, inc.at[n], shs.at[n], shr.at[n], g - 1, r)

    @pl.when(g > 0)
    def _():
        shift(0, hist.at[0]).start()

    def prep(src, dst):
        for f in range(2):
            dst[:, f * 128 + RB : (f + 1) * 128, :] = jnp.zeros((NZ, 128 - RB, 256), BF16)

        def some(i):
            blk = src[:, pl.ds(pl.multiple_of(i * 384, 128), 384)]
            hi, lo = split(jnp.concatenate([blk, jnp.zeros((128 - RB, 384), F32)], axis=0).T)
            hi, lo = hi.astype(BF16), lo.astype(BF16)
            for j in range(4):
                rows = slice((j % 2) * 128, (j % 2) * 128 + RB)
                dst[2 * i + j // 2, rows, 0:128] = hi[j * RB : (j + 1) * RB]
                dst[2 * i + j // 2, rows, 128:256] = lo[j * RB : (j + 1) * RB]

        loop(8, some)

    def prep_lags():
        def some(i):
            for a in range(2):
                blk = lagv[a, :, pl.ds(pl.multiple_of(i * 384, 128), 384)]
                for t in range(3):
                    tile = jnp.concatenate(
                        [blk[:, t * RB : (t + 1) * RB], blk[:, 288 + 32 * t : 320 + 32 * t]], axis=1
                    )
                    hi, lo = split(tile)
                    wl[i, a * RB : (a + 1) * RB, t * 128 : (t + 1) * 128] = hi.astype(BF16)
                    wl[i, (2 + a) * RB : (3 + a) * RB, t * 128 : (t + 1) * 128] = lo.astype(BF16)

        loop(8, some)

    def at_turn(k):
        return (z + (2 * (k % 2) - 1) * (8 - (k + 1) // 2) + NZ) % NZ

    def block_to(xb, par, k, f, own):
        zz = at_turn(k)
        xx = (xl + 1 - f) % 2
        v = xb.at[z, own]
        return rc(v, v, gs.at[par, 2 * k + f], gr.at[par, z * 2 + own], g, zz * 2 + xx)

    def block_from(xb, par, zz, xx):
        v = xb.at[zz, xx]
        return rc(v, v, gs.at[par, 0], gr.at[par, zz * 2 + xx], g, r)

    def send(xb, par, block, own):
        xb[z, own] = block

        def one(i):
            block_to(xb, par, i // 2, i % 2, own).start()

        loop(2 * NZ - 1, one)

    def sent(xb, par):
        loop(2 * NZ - 1, lambda i: block_to(xb, par, i // 2, i % 2, xl).wait_send())

    def arrived(xb, par, own, k):
        zz = at_turn(k)
        block_from(xb, par, zz, 1 - own).wait_recv()
        if k < NZ - 1:
            block_from(xb, par, zz, own).wait_recv()

    def product(xb, w, par=None, own=None):
        acc = [jnp.zeros((16, 256), F32), jnp.zeros((16, 256), F32)]
        for batch in ((15, 14, 13, 12, 11, 10, 9), (8, 7, 6, 5), (4, 3), (2, 1, 0)):
            if par is not None:
                for k in batch:
                    arrived(xb, par, own, k)
            for k in batch:
                zz = at_turn(k)
                x = jnp.concatenate([xb[zz, 0], xb[zz, 1]], axis=1)
                hi, lo = split(x)
                lhs = jnp.concatenate([hi, lo], axis=0).astype(BF16)
                acc[k % 2] += jnp.dot(lhs, w[zz], preferred_element_type=F32)
        acc = acc[0] + acc[1]
        return (acc[0:8, 0:128] + acc[8:16, 0:128]) + (acc[0:8, 128:256] + acc[8:16, 128:256])

    def lgather(n, pp):
        v = piece(n, c, p)
        return rc(v, v, las.at[n, pp], lar.at[n, p], pp * 2 + c, over(pp))

    def lgathered(n, pp):
        v = piece(n, c, pp)
        return rc(v, v, las.at[n, 0], lar.at[n, pp], g, r)

    def half(n, cc):
        return lb.at[n, pl.ds(pl.multiple_of(cc * HR, 8), HR), :]

    def lsib(n):
        return rc(half(n, c), half(n, c), lbs.at[n], lbr.at[n], g + 1 - 2 * c, r)

    def relay(n):
        @pl.when(g > 0)
        def _():
            lscatter(n, g).wait_recv()

        def one(i):
            pp = (p + 1 + i) % NP

            @pl.when(pp * 2 + c > 0)
            def _():
                lgather(n, pp).start()

        loop(NP - 1, one)

    def collect(n):
        @pl.when(g > 0)
        def _():
            loop(NP - 1, lambda i: lgathered(n, (p + 1 + i) % NP).wait_recv())

        @pl.when(g != 1)
        def _():
            lsib(n).start()

    def collected(n):
        @pl.when(g > 0)
        def _():
            rc(half(n, 1 - c), half(n, 1 - c), lbs.at[n], lbr.at[n], g, r).wait_recv()

    lane = lax.broadcasted_iota(jnp.int32, (8, 128), 1)

    def pack(n, i):
        last = xf[n, 2 * i + 1, 1]
        for t in range(3):
            xc[n, g, i, t] = jnp.where(
                lane < RB, xf[n, 2 * i + t // 2, t % 2], pltpu.roll(last, RB - 32 * t, 1)
            )

    def plane(n, pp):
        v = xc.at[n, g]
        return rc(v, v, pgs.at[n, pp], pgr.at[n, p], pp * 2 + c, over(pp))

    def planed(n, pp):
        v = xc.at[n, pp * 2 + c]
        return rc(v, v, pgs.at[n, 0], pgr.at[n, pp], g, r)

    def sib(n, pp):
        v = xc.at[n, pp * 2 + c]
        return rc(v, v, sgs.at[n, pp], sgr.at[n, pp], g + 1 - 2 * c, r)

    def sibbed(n, pp):
        v = xc.at[n, pp * 2 + 1 - c]
        return rc(v, v, sgs.at[n, 0], sgr.at[n, pp], g, r)

    def spread(n):
        loop(8, lambda i: pack(n, i))
        sib(n, p).start()
        loop(NP - 1, lambda i: plane(n, (p + NP - 1 - i) % NP).start())

    def forward(n):
        def one(i):
            pp = (p + 1 + i) % NP
            planed(n, pp).wait_recv()
            sib(n, pp).start()

        loop(NP - 1, one)

    def lag_part(n, i):
        x = jnp.concatenate([xc[n, :, i, t].reshape(128, 128) for t in range(3)], axis=1)
        hi, lo = split(x)
        rhs = jnp.concatenate([hi, lo], axis=0).astype(BF16)
        pa[...] += lax.dot_general(wl[i], rhs, (((1,), (1,)), ((), ())), preferred_element_type=F32)

    def lag_product(n):
        loop(NP, lambda i: sibbed(n, i).wait_recv())
        pa[...] = jnp.zeros_like(pa)
        loop(8, lambda i: lag_part(n, i))

    def turn(k):
        return (z // 2 + (1 - 2 * (k % 2)) * ((k + 1) // 2) + 8) % 8

    def qplane(i, pp):
        v = xc.at[2, g, i]
        return rc(v, v, qps.at[i, pp], qpr.at[i, p], pp * 2 + c, over(pp))

    def qplaned(i, pp):
        v = xc.at[2, pp * 2 + c, i]
        return rc(v, v, qps.at[i, 0], qpr.at[i, pp], g, r)

    def qsib(i, pp):
        v = xc.at[2, pp * 2 + c, i]
        return rc(v, v, qss.at[i, pp], qsr.at[i, pp], g + 1 - 2 * c, r)

    def qsibbed(i, pp):
        v = xc.at[2, pp * 2 + 1 - c, i]
        return rc(v, v, qss.at[i, 0], qsr.at[i, pp], g, r)

    def qspread(k):
        i = turn(k)
        pack(2, i)
        loop(NP - 1, lambda j: qplane(i, (p + NP - 1 - j) % NP).start())
        qsib(i, p).start()

    def qblock(zz, xx):
        @pl.when((zz != z) | (xx != xl))
        def _():
            block_from(xf.at[2], 1, zz, xx).wait_recv()

    def qgather(k):
        for j in range(4):
            qblock(2 * turn(k) + j // 2, j % 2)
        qspread(k)

    def qforward(k):
        i = turn(k)

        def one(j):
            pp = (p + 1 + j) % NP
            qplaned(i, pp).wait_recv()
            qsib(i, pp).start()

        loop(NP - 1, one)

    def qproduct(k):
        i = turn(k)
        loop(NP, lambda j: qsibbed(i, j).wait_recv())
        lag_part(2, i)

    def lag_rows(a):
        lo, hi = a * RB, (a + 1) * RB
        big = pa[lo:hi, 0:128] + pa[lo:hi, 128:256]
        small = pa[2 * RB + lo : 2 * RB + hi, 0:128] + pa[2 * RB + lo : 2 * RB + hi, 128:256]
        return big + small

    def incoming(n):
        @pl.when(g < NG - 1)
        def _():
            rc(inc.at[n], inc.at[n], shs.at[n], shr.at[n], g, r).wait_recv()

        @pl.when(g == NG - 1)
        def _():
            inc[n] = jnp.zeros((RB, 128), F32)

    def advance(n):
        lag_product(n)
        incoming(n)
        first = hist[1] if n == 0 else accs[n - 1, 1]
        accs[n, 0] = first + lag_rows(0)
        accs[n, 1] = inc[n] + lag_rows(1)

        @pl.when(g > 0)
        def _():
            shift(n + 1, accs.at[n, 0]).start()

    loc[0].wait()
    prep(invv, wv)
    loc[1].wait()

    def rwait(n):
        @pl.when(g != n // 2)
        def _():
            rscatter(n, g).wait_recv()

    rwait(0)
    send(xr.at[0], 0, rbuf[0], rx)
    relay(0)

    @pl.when(g == 0)
    def _():
        loop(NG - 1, lambda i: lscatter(1, NG - 1 - i).start())

    now = product(xr.at[0], wv, 0, rx)
    send(xf.at[0], 1, now, xl)
    sent(xr.at[0], 0)
    collect(0)
    relay(1)
    collected(0)
    prep(lb.at[0], w0)
    rwait(1)
    now = rbuf[1] - product(xf.at[0], w0, 1, xl)
    send(xr.at[1], 0, now, rx)
    spread(0)
    sent(xf.at[0], 1)
    prep_lags()
    collect(1)
    now = product(xr.at[1], wv, 0, rx)
    send(xf.at[1], 1, now, xl)
    sent(xr.at[1], 0)
    collected(1)
    prep(lb.at[1], w1)
    rwait(2)
    late = rbuf[2] - product(xf.at[0], w1)
    forward(0)
    now = late - product(xf.at[1], w0, 1, xl)
    send(xr.at[2], 0, now, rx)
    spread(1)
    sent(xf.at[1], 1)
    advance(0)
    now = product(xr.at[2], wv, 0, rx)
    send(xf.at[2], 1, now, xl)
    sent(xr.at[2], 0)
    loop(3, qgather)
    forward(1)
    loop(5, lambda k: qgather(k + 3))
    sent(xf.at[2], 1)
    advance(1)
    pa[...] = jnp.zeros_like(pa)
    qforward(0)

    def last(k):
        qforward(k + 1)
        qproduct(k)

    loop(7, last)
    m = z // 2
    own = 2 * (z % 2) + xl

    @pl.when(own < 3)
    def _():
        cur_ref[...] = xc[2, :, m, own].reshape(128, 128).T[0:RB]

    @pl.when(own == 3)
    def _():
        for t in range(3):
            cur_ref[32 * t : 32 * t + 32] = xc[2, :, m, t].reshape(128, 128).T[RB:128]

    incoming(2)
    qproduct(7)
    fut_ref[0] = accs[1, 1] + lag_rows(0)
    fut_ref[1] = inc[2] + lag_rows(1)

    @pl.when(g == 0)
    def _():
        for n in range(2):
            loop(NG - 1, lambda i, n=n: rscatter(n, 1 + i).wait_send())
            loop(NG - 1, lambda i, n=n: lscatter(n, 1 + i).wait_send())

    @pl.when(g == 1)
    def _():
        loop(NG - 1, lambda i: rscatter(2, (g + 1 + i) % NG).wait_send())

    for n in range(2):

        def lsent(i, n=n):
            pp = (p + 1 + i) % NP

            @pl.when(pp * 2 + c > 0)
            def _():
                lgather(n, pp).wait_send()

        loop(NP - 1, lsent)

        @pl.when(g != 1)
        def _(n=n):
            lsib(n).wait_send()

    def qsent(i):
        loop(NP - 1, lambda j: qplane(i, (p + 1 + j) % NP).wait_send())
        loop(NP, lambda j: qsib(i, j).wait_send())

    loop(8, qsent)
    for n in range(3):
        if n < 2:
            loop(NP - 1, lambda i, n=n: plane(n, (p + 1 + i) % NP).wait_send())
            loop(NP, lambda i, n=n: sib(n, i).wait_send())

        @pl.when(g > 0)
        def _(n=n):
            shift(n, accs.at[0, 0]).wait_send()


def body(lag_ops, inverse, history, loads):
    anyspec = pl.BlockSpec(memory_space=pl.ANY)
    vspec = pl.BlockSpec(memory_space=pltpu.VMEM)
    dma = pltpu.SemaphoreType.DMA
    scratch = [
        pltpu.VMEM((2, RB, U), F32),
        pltpu.VMEM((RB, U), F32),
        pltpu.VMEM((2, RB, 128), F32),
        pltpu.VMEM((3, RB, 128), F32),
        pltpu.VMEM((2, RB, U), F32),
        pltpu.VMEM((NZ, 256, 256), BF16),
        pltpu.VMEM((NZ, 256, 256), BF16),
        pltpu.VMEM((NZ, 256, 256), BF16),
        pltpu.VMEM((8, 4 * RB, 384), BF16),
        pltpu.VMEM((3, NZ, 2, 8, 128), F32),
        pltpu.VMEM((3, NZ, 2, 8, 128), F32),
        pltpu.VMEM((3, NG, 8, 3, 8, 128), F32),
        pltpu.VMEM((3, NG, 8, 128), F32),
        pltpu.VMEM((3, 8, 128), F32),
        pltpu.VMEM((3, RB, 128), F32),
        pltpu.VMEM((2, 2, RB, 128), F32),
        pltpu.VMEM((4 * RB, 256), F32),
        dma((5,)),
        dma((2, 2 * NZ)),
        dma((2, 2 * NZ)),
        dma((3, NG)),
        dma((3,)),
        dma((2, NG)),
        dma((2,)),
        dma((2, NP)),
        dma((2, NP)),
        dma((2,)),
        dma((2,)),
        dma((2, NP)),
        dma((2, NP)),
        dma((2, NP)),
        dma((2, NP)),
        dma((3,)),
        dma((3,)),
        dma((8, NP)),
        dma((8, NP)),
        dma((8, NP)),
        dma((8, NP)),
    ]
    return pl.pallas_call(
        kernel,
        out_shape=(
            jax.ShapeDtypeStruct((RB, 128), F32),
            jax.ShapeDtypeStruct((2, RB, 128), F32),
        ),
        in_specs=[anyspec] * 4,
        out_specs=(vspec, vspec),
        scratch_shapes=scratch,
        compiler_params=pltpu.CompilerParams(
            collective_id=0, has_side_effects=True, vmem_limit_bytes=60 * 2**20
        ),
    )(lag_ops, inverse, history, loads)


def solution(mesh):
    placed = (P("lag", "row", None), P("row", None), P("lag", "row", None), P(None, "row", None))
    return jax.shard_map(
        body,
        mesh=mesh,
        in_specs=placed,
        out_specs=(P("row", None), P("lag", "row", None)),
        check_vma=False,
    )
```

```python
import functools

import jax
import jax.numpy as jnp
from jax import lax
from jax.experimental import pallas as pl
from jax.experimental.pallas import tpu as pltpu
from jax.sharding import PartitionSpec as P

MESH = pl.DeviceIdType.MESH
F32 = jnp.float32
BF16 = jnp.bfloat16
NG = 16
NP = 8
NZ = 16
RB = 96
U = 3072
PC = U // NP
HR = RB // 2


def split(x):
    hi = x.astype(BF16).astype(F32)
    return hi, x - hi


def kernel(
    lag_h, inv_h, hist_h, loads_h, cur_ref, fut_ref,
    lagv, invv, hist, loads, lb, wv, w0, w1, wl, xr, xf, xc, tbuf, rbuf, inc, accs, pa,
    lsem, gs, gr, rss, rsr, lss, lsr, las, lar, lbs, lbr, pgs, pgr, sgs, sgr, shs, shr, qps, qpr, qss, qsr,
):
    g = lax.axis_index("lag")
    r = lax.axis_index("row")
    z, xl = r // 2, r % 2
    p, c = g // 2, g % 2
    xh = p % 2
    rx = (xl + xh) % 2

    def rc(src, dst, ss, rs, gg, rr):
        return pltpu.make_async_remote_copy(
            src_ref=src, dst_ref=dst, send_sem=ss, recv_sem=rs, device_id=(gg, rr), device_id_type=MESH
        )

    def loop(n, f):
        lax.fori_loop(0, n, lambda i, _: (f(i), 0)[1], 0)

    def over(pp):
        return z * 2 + (xl + xh + pp) % 2

    barrier = pltpu.get_barrier_semaphore()

    def greet(gg, rr):
        pl.semaphore_signal(barrier, inc=1, device_id=(gg, rr), device_id_type=MESH)

    loop(2 * NZ - 1, lambda i: greet(g, (r + 1 + i) % (2 * NZ)))
    loop(NG - 1, lambda i: greet((g + 1 + i) % NG, over((g + 1 + i) % NG // 2)))

    @pl.when((g > 0) & ((g - 1) // 2 % 2 != xh))
    def _():
        greet(g - 1, r)

    @pl.when((g < NG - 1) & ((g + 1) // 2 % 2 != xh))
    def _():
        greet(g + 1, r)

    extra = jnp.where((g > 0) & (g % 2 == 0), 1, 0) + jnp.where((g < NG - 1) & (g % 2 == 1), 1, 0)

    loc = [
        pltpu.make_async_copy(inv_h, invv, lsem.at[0]),
        pltpu.make_async_copy(lag_h, lagv, lsem.at[1]),
        pltpu.make_async_copy(hist_h, hist, lsem.at[2]),
        pltpu.make_async_copy(loads_h, loads, lsem.at[3]),
    ]
    for cp in (loc[3], loc[2], loc[0], loc[1]):
        cp.start()
    root = pltpu.make_async_copy(lag_h, lb, lsem.at[4])

    @pl.when(g == 0)
    def _():
        root.start()

    loc[3].wait()
    loc[2].wait()

    def turned(n, h):
        d = loads[n] - hist[h]
        return jnp.concatenate([d, jnp.zeros((128 - RB, 128), F32)], axis=0).T.reshape(NG, 8, 128)

    @pl.when(g == 0)
    def _():
        t0 = turned(0, 0)
        tbuf[0] = t0
        rbuf[0] = t0[0]
        t1 = turned(1, 1)
        tbuf[1] = t1
        rbuf[1] = t1[0]
        root.wait()

    @pl.when(g == 1)
    def _():
        t2 = turned(2, 0)
        tbuf[2] = t2
        rbuf[2] = t2[1]

    pl.semaphore_wait(barrier, 2 * NZ - 1 + NG - 1 + extra)

    def rscatter(n, gg):
        return rc(tbuf.at[n, gg], rbuf.at[n], rss.at[n, gg], rsr.at[n], gg, over(gg // 2))

    def piece(n, cc, pp):
        return lb.at[n, pl.ds(pl.multiple_of(cc * HR, 8), HR), pl.ds(pl.multiple_of(pp * PC, 128), PC)]

    def lscatter(n, gg):
        v = piece(n, gg % 2, gg // 2)
        return rc(v, v, lss.at[n, gg], lsr.at[n], gg, over(gg // 2))

    @pl.when(g == 0)
    def _():
        loop(NG - 1, lambda i: rscatter(0, NG - 1 - i).start())
        loop(NG - 2, lambda i: lscatter(0, NG - 1 - i).start())
        loop(NG - 1, lambda i: rscatter(1, NG - 1 - i).start())

    @pl.when(g == 1)
    def _():
        loop(NG - 1, lambda i: rscatter(2, (g + 1 + i) % NG).start())

    def shift(n, src):
        return rc(src, inc.at[n], shs.at[n], shr.at[n], g - 1, r)

    @pl.when(g > 0)
    def _():
        shift(0, hist.at[0]).start()

    def prep_zero(dst):
        for f in range(2):
            dst[:, f * 128 + RB : (f + 1) * 128, :] = jnp.zeros((NZ, 128 - RB, 256), BF16)

    def turned_parts(blk):
        hi, lo = split(jnp.concatenate([blk, jnp.zeros((128 - RB, 384), F32)], axis=0).T)
        return hi.astype(BF16), lo.astype(BF16)

    def prep(src, dst, i):
        hi, lo = turned_parts(src[:, pl.ds(pl.multiple_of(i * 384, 128), 384)])
        for j in range(4):
            rows = slice((j % 2) * 128, (j % 2) * 128 + RB)
            dst[2 * i + j // 2, rows, 0:128] = hi[j * RB : (j + 1) * RB]
            dst[2 * i + j // 2, rows, 128:256] = lo[j * RB : (j + 1) * RB]

    def prep_lags():
        def some(i):
            for a in range(2):
                hi, lo = turned_parts(lagv[a, :, pl.ds(pl.multiple_of(i * 384, 128), 384)])
                for part, n in ((hi, a * 128), (lo, 256 + a * 128)):
                    for t in range(3):
                        wl[i, t * 128 : t * 128 + RB, n : n + 128] = part[t * RB : (t + 1) * RB]
                        wl[i, t * 128 + RB : (t + 1) * 128, n : n + 128] = part[288 + 32 * t : 320 + 32 * t]

        loop(8, some)

    def at_turn(k):
        return (z + (2 * (k % 2) - 1) * (8 - (k + 1) // 2) + NZ) % NZ

    def block_to(xb, par, k, f, own):
        zz = at_turn(k)
        xx = (xl + 1 - f) % 2
        v = xb.at[z, own]
        return rc(v, v, gs.at[par, 2 * k + f], gr.at[par, z * 2 + own], g, zz * 2 + xx)

    def block_from(xb, par, zz, xx):
        v = xb.at[zz, xx]
        return rc(v, v, gs.at[par, 0], gr.at[par, zz * 2 + xx], g, r)

    def send(xb, par, block, own):
        xb[z, own] = block

        def one(i):
            block_to(xb, par, i // 2, i % 2, own).start()

        loop(2 * NZ - 1, one)

    def send_near(xb, par, block, own):
        xb[z, own] = block
        block_to(xb, par, 0, 0, own).start()
        block_to(xb, par, 0, 1, own).start()

        def one(i):
            j = 2 * NZ - 2 - i
            block_to(xb, par, j // 2, j % 2, own).start()

        loop(2 * NZ - 3, one)

    def sent(xb, par):
        loop(2 * NZ - 1, lambda i: block_to(xb, par, i // 2, i % 2, xl).wait_send())

    def arrived(xb, par, own, k):
        zz = at_turn(k)
        block_from(xb, par, zz, 1 - own).wait_recv()
        if k < NZ - 1:
            block_from(xb, par, zz, own).wait_recv()

    def product(xb, w, par=None, own=None):
        acc = [jnp.zeros((16, 256), F32), jnp.zeros((16, 256), F32)]
        for batch in ((15, 14, 13, 12, 11, 10, 9), (8, 7, 6, 5), (4, 3), (2, 1, 0)):
            if par is not None:
                for k in batch:
                    arrived(xb, par, own, k)
            for k in batch:
                zz = at_turn(k)
                x = jnp.concatenate([xb[zz, 0], xb[zz, 1]], axis=1)
                hi, lo = split(x)
                lhs = jnp.concatenate([hi, lo], axis=0).astype(BF16)
                acc[k % 2] += jnp.dot(lhs, w[zz], preferred_element_type=F32)
        acc = acc[0] + acc[1]
        return (acc[0:8, 0:128] + acc[8:16, 0:128]) + (acc[0:8, 128:256] + acc[8:16, 128:256])

    def lgather(n, pp):
        v = piece(n, c, p)
        return rc(v, v, las.at[n, pp], lar.at[n, p], pp * 2 + c, over(pp))

    def lgathered(n, pp):
        v = piece(n, c, pp)
        return rc(v, v, las.at[n, 0], lar.at[n, pp], g, r)

    def lsib(n, pp):
        v = piece(n, c, pp)
        return rc(v, v, lbs.at[n, pp], lbr.at[n, pp], g + 1 - 2 * c, r)

    def lsibbed(n, pp):
        v = piece(n, 1 - c, pp)
        return rc(v, v, lbs.at[n, 0], lbr.at[n, pp], g, r)

    def relay(n):
        @pl.when(g > 0)
        def _():
            lscatter(n, g).wait_recv()

        def one(i):
            pp = (p + 1 + i) % NP

            @pl.when(pp * 2 + c > 0)
            def _():
                lgather(n, pp).start()

        loop(NP - 1, one)

        @pl.when(g != 1)
        def _():
            lsib(n, p).start()

    def collect(n):
        def one(i):
            pp = (p + 1 + i) % NP

            @pl.when(g > 0)
            def _():
                lgathered(n, pp).wait_recv()

            @pl.when(g != 1)
            def _():
                lsib(n, pp).start()

        loop(NP - 1, one)

    def prepare(n, dst):
        def one(i):
            pp = (p + i) % NP

            @pl.when(g > 0)
            def _():
                lsibbed(n, pp).wait_recv()

            prep(lb.at[n], dst, pp)

        loop(NP, one)

    lane = lax.broadcasted_iota(jnp.int32, (8, 128), 1)

    def pack(n, i):
        last = xf[n, 2 * i + 1, 1]
        for t in range(3):
            xc[n, g, i, t] = jnp.where(
                lane < RB, xf[n, 2 * i + t // 2, t % 2], pltpu.roll(last, RB - 32 * t, 1)
            )

    def plane(n, pp):
        v = xc.at[n, g]
        return rc(v, v, pgs.at[n, pp], pgr.at[n, p], pp * 2 + c, over(pp))

    def planed(n, pp):
        v = xc.at[n, pp * 2 + c]
        return rc(v, v, pgs.at[n, 0], pgr.at[n, pp], g, r)

    def sib(n, pp):
        v = xc.at[n, pp * 2 + c]
        return rc(v, v, sgs.at[n, pp], sgr.at[n, pp], g + 1 - 2 * c, r)

    def sibbed(n, pp):
        v = xc.at[n, pp * 2 + 1 - c]
        return rc(v, v, sgs.at[n, 0], sgr.at[n, pp], g, r)

    def spread(n):
        loop(8, lambda i: pack(n, i))
        sib(n, p).start()
        loop(NP - 1, lambda i: plane(n, (p + NP - 1 - i) % NP).start())

    def forward(n):
        def one(i):
            pp = (p + 1 + i) % NP
            planed(n, pp).wait_recv()
            sib(n, pp).start()

        loop(NP - 1, one)

    def lag_part(n, i):
        x = jnp.concatenate([xc[n, :, i, t].reshape(128, 128) for t in range(3)], axis=1)
        hi, lo = split(x)
        lhs = jnp.concatenate([hi, lo], axis=0).astype(BF16)
        o = jnp.dot(lhs, wl[i], preferred_element_type=F32)
        pa[...] += (o[0:128, 0:256] + o[128:256, 0:256]) + (o[0:128, 256:512] + o[128:256, 256:512])

    def lag_product(n):
        loop(NP, lambda i: sibbed(n, i).wait_recv())
        pa[...] = jnp.zeros_like(pa)
        loop(8, lambda i: lag_part(n, i))

    def turn(k):
        return (z // 2 + (1 - 2 * (k % 2)) * ((k + 1) // 2) + 8) % 8

    def qplane(i, pp):
        v = xc.at[2, g, i]
        return rc(v, v, qps.at[i, pp], qpr.at[i, p], pp * 2 + c, over(pp))

    def qplaned(i, pp):
        v = xc.at[2, pp * 2 + c, i]
        return rc(v, v, qps.at[i, 0], qpr.at[i, pp], g, r)

    def qsib(i, pp):
        v = xc.at[2, pp * 2 + c, i]
        return rc(v, v, qss.at[i, pp], qsr.at[i, pp], g + 1 - 2 * c, r)

    def qsibbed(i, pp):
        v = xc.at[2, pp * 2 + 1 - c, i]
        return rc(v, v, qss.at[i, 0], qsr.at[i, pp], g, r)

    def qspread(k):
        i = turn(k)
        pack(2, i)
        loop(NP - 1, lambda j: qplane(i, (p + NP - 1 - j) % NP).start())
        qsib(i, p).start()

    def qblock(zz, xx):
        @pl.when((zz != z) | (xx != xl))
        def _():
            block_from(xf.at[2], 1, zz, xx).wait_recv()

    def qgather(k):
        for j in range(4):
            qblock(2 * turn(k) + j // 2, j % 2)
        qspread(k)

    def qforward(k):
        i = turn(k)

        def one(j):
            pp = (p + 1 + j) % NP
            qplaned(i, pp).wait_recv()
            qsib(i, pp).start()

        loop(NP - 1, one)

    def qproduct(k):
        i = turn(k)
        loop(NP, lambda j: qsibbed(i, j).wait_recv())
        lag_part(2, i)

    def lag_rows(a):
        return pa[:, a * 128 : (a + 1) * 128].T[0:RB]

    def incoming(n):
        @pl.when(g < NG - 1)
        def _():
            rc(inc.at[n], inc.at[n], shs.at[n], shr.at[n], g, r).wait_recv()

        @pl.when(g == NG - 1)
        def _():
            inc[n] = jnp.zeros((RB, 128), F32)

    def advance(n):
        lag_product(n)
        incoming(n)
        first = hist[1] if n == 0 else accs[n - 1, 1]
        accs[n, 0] = first + lag_rows(0)
        accs[n, 1] = inc[n] + lag_rows(1)

        @pl.when(g > 0)
        def _():
            shift(n + 1, accs.at[n, 0]).start()

    prep_zero(wv)
    loc[0].wait()
    loop(8, lambda i: prep(invv, wv, i))
    for w in (w0, w1):
        prep_zero(w)
    loc[1].wait()

    def rwait(n):
        @pl.when(g != n // 2)
        def _():
            rscatter(n, g).wait_recv()

    rwait(0)
    send(xr.at[0], 0, rbuf[0], rx)

    @pl.when(g == 0)
    def _():
        loop(NG - 2, lambda i: lscatter(0, NG - 1 - i).wait_send())
        lscatter(0, 1).start()

    relay(0)
    now = product(xr.at[0], wv, 0, rx)
    send(xf.at[0], 1, now, xl)
    sent(xr.at[0], 0)

    @pl.when(g == 0)
    def _():
        loop(NG - 1, lambda i: lscatter(1, NG - 1 - i).start())

    collect(0)
    prepare(0, w0)
    rwait(1)
    now = rbuf[1] - product(xf.at[0], w0, 1, xl)
    send(xr.at[1], 0, now, rx)
    relay(1)
    sent(xf.at[0], 1)
    prep_lags()
    now = product(xr.at[1], wv, 0, rx)
    send(xf.at[1], 1, now, xl)
    spread(0)
    sent(xr.at[1], 0)
    collect(1)
    prepare(1, w1)
    rwait(2)
    late = rbuf[2] - product(xf.at[0], w1)
    now = late - product(xf.at[1], w0, 1, xl)
    send(xr.at[2], 0, now, rx)
    spread(1)
    sent(xf.at[1], 1)
    forward(0)
    advance(0)
    now = product(xr.at[2], wv, 0, rx)
    send_near(xf.at[2], 1, now, xl)
    sent(xr.at[2], 0)
    loop(3, qgather)
    forward(1)
    loop(5, lambda k: qgather(k + 3))
    sent(xf.at[2], 1)
    advance(1)
    pa[...] = jnp.zeros_like(pa)
    qforward(0)

    def last(k):
        qforward(k + 1)
        qproduct(k)

    loop(7, last)
    m = z // 2
    own = 2 * (z % 2) + xl

    @pl.when(own < 3)
    def _():
        cur_ref[...] = xc[2, :, m, own].reshape(128, 128).T[0:RB]

    @pl.when(own == 3)
    def _():
        for t in range(3):
            cur_ref[32 * t : 32 * t + 32] = xc[2, :, m, t].reshape(128, 128).T[RB:128]

    incoming(2)
    qproduct(7)
    fut_ref[0] = accs[1, 1] + lag_rows(0)
    fut_ref[1] = inc[2] + lag_rows(1)

    @pl.when(g == 0)
    def _():
        for n in range(2):
            loop(NG - 1, lambda i, n=n: rscatter(n, 1 + i).wait_send())
            loop(NG - 1 if n else 1, lambda i, n=n: lscatter(n, 1 + i).wait_send())

    @pl.when(g == 1)
    def _():
        loop(NG - 1, lambda i: rscatter(2, (g + 1 + i) % NG).wait_send())

    for n in range(2):

        def lsent(i, n=n):
            pp = (p + 1 + i) % NP

            @pl.when(pp * 2 + c > 0)
            def _():
                lgather(n, pp).wait_send()

        loop(NP - 1, lsent)

        @pl.when(g != 1)
        def _(n=n):
            loop(NP, lambda i: lsib(n, i).wait_send())

    def qsent(i):
        loop(NP - 1, lambda j: qplane(i, (p + 1 + j) % NP).wait_send())
        loop(NP, lambda j: qsib(i, j).wait_send())

    loop(8, qsent)
    for n in range(3):
        if n < 2:
            loop(NP - 1, lambda i, n=n: plane(n, (p + 1 + i) % NP).wait_send())
            loop(NP, lambda i, n=n: sib(n, i).wait_send())

        @pl.when(g > 0)
        def _(n=n):
            shift(n, accs.at[0, 0]).wait_send()


def body(lag_ops, inverse, history, loads):
    anyspec = pl.BlockSpec(memory_space=pl.ANY)
    vspec = pl.BlockSpec(memory_space=pltpu.VMEM)
    dma = pltpu.SemaphoreType.DMA
    scratch = [
        pltpu.VMEM((2, RB, U), F32),
        pltpu.VMEM((RB, U), F32),
        pltpu.VMEM((2, RB, 128), F32),
        pltpu.VMEM((3, RB, 128), F32),
        pltpu.VMEM((2, RB, U), F32),
        pltpu.VMEM((NZ, 256, 256), BF16),
        pltpu.VMEM((NZ, 256, 256), BF16),
        pltpu.VMEM((NZ, 256, 256), BF16),
        pltpu.VMEM((8, 384, 512), BF16),
        pltpu.VMEM((3, NZ, 2, 8, 128), F32),
        pltpu.VMEM((3, NZ, 2, 8, 128), F32),
        pltpu.VMEM((3, NG, 8, 3, 8, 128), F32),
        pltpu.VMEM((3, NG, 8, 128), F32),
        pltpu.VMEM((3, 8, 128), F32),
        pltpu.VMEM((3, RB, 128), F32),
        pltpu.VMEM((2, 2, RB, 128), F32),
        pltpu.VMEM((128, 256), F32),
        dma((5,)),
        dma((2, 2 * NZ)),
        dma((2, 2 * NZ)),
        dma((3, NG)),
        dma((3,)),
        dma((2, NG)),
        dma((2,)),
        dma((2, NP)),
        dma((2, NP)),
        dma((2, NP)),
        dma((2, NP)),
        dma((2, NP)),
        dma((2, NP)),
        dma((2, NP)),
        dma((2, NP)),
        dma((3,)),
        dma((3,)),
        dma((8, NP)),
        dma((8, NP)),
        dma((8, NP)),
        dma((8, NP)),
    ]
    return pl.pallas_call(
        kernel,
        out_shape=(
            pltpu.VMEM((RB, 128), F32),
            pltpu.VMEM((2, RB, 128), F32),
        ),
        in_specs=[anyspec] * 4,
        out_specs=(vspec, vspec),
        scratch_shapes=scratch,
        compiler_params=pltpu.CompilerParams(
            collective_id=0, has_side_effects=True, vmem_limit_bytes=60 * 2**20
        ),
    )(lag_ops, inverse, history, loads)


def solution(mesh):
    placed = (P("lag", "row", None), P("row", None), P("lag", "row", None), P(None, "row", None))
    return jax.shard_map(
        body,
        mesh=mesh,
        in_specs=placed,
        out_specs=(P("row", None), P("lag", "row", None)),
        check_vma=False,
    )
```

```python
import functools

import jax
import jax.numpy as jnp
from jax import lax
from jax.experimental import pallas as pl
from jax.experimental.pallas import tpu as pltpu
from jax.sharding import PartitionSpec as P

MESH = pl.DeviceIdType.MESH
F32 = jnp.float32
BF16 = jnp.bfloat16
NG = 16
NP = 8
NZ = 16
RB = 96
U = 3072
PC = U // NP
HR = RB // 2


def split(x):
    hi = x.astype(BF16).astype(F32)
    return hi, x - hi


def kernel(
    lag_h, inv_h, hist_h, loads_h, cur_ref, fut_ref,
    lagv, invv, hist, loads, lb, wv, w0, w1, wl, xr, xf, xc, tbuf, rbuf, inc, accs, pa,
    lsem, gs, gr, rss, rsr, lss, lsr, las, lar, lbs, lbr, pgs, pgr, sgs, sgr, shs, shr, qps, qpr, qss, qsr,
):
    g = lax.axis_index("lag")
    r = lax.axis_index("row")
    z, xl = r // 2, r % 2
    p, c = g // 2, g % 2
    xh = p % 2
    rx = (xl + xh) % 2

    def rc(src, dst, ss, rs, gg, rr):
        return pltpu.make_async_remote_copy(
            src_ref=src, dst_ref=dst, send_sem=ss, recv_sem=rs, device_id=(gg, rr), device_id_type=MESH
        )

    def loop(n, f):
        lax.fori_loop(0, n, lambda i, _: (f(i), 0)[1], 0)

    def over(pp):
        return z * 2 + (xl + xh + pp) % 2

    barrier = pltpu.get_barrier_semaphore()

    def greet(gg, rr):
        pl.semaphore_signal(barrier, inc=1, device_id=(gg, rr), device_id_type=MESH)

    loop(2 * NZ - 1, lambda i: greet(g, (r + 1 + i) % (2 * NZ)))
    loop(NG - 1, lambda i: greet((g + 1 + i) % NG, over((g + 1 + i) % NG // 2)))

    @pl.when((g > 0) & ((g - 1) // 2 % 2 != xh))
    def _():
        greet(g - 1, r)

    @pl.when((g < NG - 1) & ((g + 1) // 2 % 2 != xh))
    def _():
        greet(g + 1, r)

    extra = jnp.where((g > 0) & (g % 2 == 0), 1, 0) + jnp.where((g < NG - 1) & (g % 2 == 1), 1, 0)

    loc = [
        pltpu.make_async_copy(inv_h, invv, lsem.at[0]),
        pltpu.make_async_copy(lag_h, lagv, lsem.at[1]),
        pltpu.make_async_copy(hist_h, hist, lsem.at[2]),
        pltpu.make_async_copy(loads_h, loads, lsem.at[3]),
    ]
    for cp in (loc[3], loc[2], loc[0], loc[1]):
        cp.start()
    root = pltpu.make_async_copy(lag_h, lb, lsem.at[4])

    @pl.when(g == 0)
    def _():
        root.start()

    loc[3].wait()
    loc[2].wait()

    def turned(n, h):
        d = loads[n] - hist[h]
        return jnp.concatenate([d, jnp.zeros((128 - RB, 128), F32)], axis=0).T.reshape(NG, 8, 128)

    @pl.when(g == 0)
    def _():
        t0 = turned(0, 0)
        tbuf[0] = t0
        rbuf[0] = t0[0]
        t1 = turned(1, 1)
        tbuf[1] = t1
        rbuf[1] = t1[0]
        root.wait()

    @pl.when(g == 1)
    def _():
        t2 = turned(2, 0)
        tbuf[2] = t2
        rbuf[2] = t2[1]

    pl.semaphore_wait(barrier, 2 * NZ - 1 + NG - 1 + extra)

    def rscatter(n, gg):
        return rc(tbuf.at[n, gg], rbuf.at[n], rss.at[n, gg], rsr.at[n], gg, over(gg // 2))

    def piece(n, cc, pp):
        return lb.at[n, pl.ds(pl.multiple_of(cc * HR, 8), HR), pl.ds(pl.multiple_of(pp * PC, 128), PC)]

    def lscatter(n, gg):
        v = piece(n, gg % 2, gg // 2)
        return rc(v, v, lss.at[n, gg], lsr.at[n], gg, over(gg // 2))

    @pl.when(g == 0)
    def _():
        loop(NG - 1, lambda i: rscatter(0, NG - 1 - i).start())
        loop(NG - 2, lambda i: lscatter(0, NG - 1 - i).start())
        loop(NG - 1, lambda i: rscatter(1, NG - 1 - i).start())

    @pl.when(g == 1)
    def _():
        loop(NG - 1, lambda i: rscatter(2, (g + 1 + i) % NG).start())

    def shift(n, src):
        return rc(src, inc.at[n], shs.at[n], shr.at[n], g - 1, r)

    @pl.when(g > 0)
    def _():
        shift(0, hist.at[0]).start()

    def prep_zero(dst):
        for f in range(2):
            dst[:, f * 128 + RB : (f + 1) * 128, :] = jnp.zeros((NZ, 128 - RB, 256), BF16)

    def turned_parts(blk):
        hi, lo = split(jnp.concatenate([blk, jnp.zeros((128 - RB, 384), F32)], axis=0).T)
        return hi.astype(BF16), lo.astype(BF16)

    def prep(src, dst, i):
        hi, lo = turned_parts(src[:, pl.ds(pl.multiple_of(i * 384, 128), 384)])
        for j in range(4):
            rows = slice((j % 2) * 128, (j % 2) * 128 + RB)
            dst[2 * i + j // 2, rows, 0:128] = hi[j * RB : (j + 1) * RB]
            dst[2 * i + j // 2, rows, 128:256] = lo[j * RB : (j + 1) * RB]

    def prep_lags():
        def some(i):
            for a in range(2):
                hi, lo = turned_parts(lagv[a, :, pl.ds(pl.multiple_of(i * 384, 128), 384)])
                for part, n in ((hi, a * 128), (lo, 256 + a * 128)):
                    for t in range(3):
                        wl[i, t * 128 : t * 128 + RB, n : n + 128] = part[t * RB : (t + 1) * RB]
                        wl[i, t * 128 + RB : (t + 1) * 128, n : n + 128] = part[288 + 32 * t : 320 + 32 * t]

        loop(8, some)

    def at_turn(k):
        return (z + (2 * (k % 2) - 1) * (8 - (k + 1) // 2) + NZ) % NZ

    def block_to(xb, par, k, f, own):
        zz = at_turn(k)
        xx = (xl + 1 - f) % 2
        v = xb.at[z, own]
        return rc(v, v, gs.at[par, 2 * k + f], gr.at[par, z * 2 + own], g, zz * 2 + xx)

    def block_from(xb, par, zz, xx):
        v = xb.at[zz, xx]
        return rc(v, v, gs.at[par, 0], gr.at[par, zz * 2 + xx], g, r)

    def send(xb, par, block, own):
        xb[z, own] = block

        def one(i):
            block_to(xb, par, i // 2, i % 2, own).start()

        loop(2 * NZ - 1, one)

    def send_near(xb, par, block, own):
        xb[z, own] = block
        block_to(xb, par, 0, 0, own).start()
        block_to(xb, par, 0, 1, own).start()

        def one(i):
            j = 2 * NZ - 2 - i
            block_to(xb, par, j // 2, j % 2, own).start()

        loop(2 * NZ - 3, one)

    def sent(xb, par):
        loop(2 * NZ - 1, lambda i: block_to(xb, par, i // 2, i % 2, xl).wait_send())

    def arrived(xb, par, own, k):
        zz = at_turn(k)
        block_from(xb, par, zz, 1 - own).wait_recv()
        if k < NZ - 1:
            block_from(xb, par, zz, own).wait_recv()

    def product(xb, w, par=None, own=None):
        acc = [jnp.zeros((16, 256), F32), jnp.zeros((16, 256), F32)]
        for batch in ((15, 14, 13, 12, 11, 10, 9), (8, 7, 6, 5), (4, 3), (2, 1, 0)):
            if par is not None:
                for k in batch:
                    arrived(xb, par, own, k)
            for k in batch:
                zz = at_turn(k)
                x = jnp.concatenate([xb[zz, 0], xb[zz, 1]], axis=1)
                hi, lo = split(x)
                lhs = jnp.concatenate([hi, lo], axis=0).astype(BF16)
                acc[k % 2] += jnp.dot(lhs, w[zz], preferred_element_type=F32)
        acc = acc[0] + acc[1]
        return (acc[0:8, 0:128] + acc[8:16, 0:128]) + (acc[0:8, 128:256] + acc[8:16, 128:256])

    def lgather(n, pp):
        v = piece(n, c, p)
        return rc(v, v, las.at[n, pp], lar.at[n, p], pp * 2 + c, over(pp))

    def lgathered(n, pp):
        v = piece(n, c, pp)
        return rc(v, v, las.at[n, 0], lar.at[n, pp], g, r)

    def lsib(n, pp):
        v = piece(n, c, pp)
        return rc(v, v, lbs.at[n, pp], lbr.at[n, pp], g + 1 - 2 * c, r)

    def lsibbed(n, pp):
        v = piece(n, 1 - c, pp)
        return rc(v, v, lbs.at[n, 0], lbr.at[n, pp], g, r)

    def relay(n):
        @pl.when(g > 0)
        def _():
            lscatter(n, g).wait_recv()

        def one(i):
            pp = (p + 1 + i) % NP

            @pl.when(pp * 2 + c > 0)
            def _():
                lgather(n, pp).start()

        loop(NP - 1, one)

        @pl.when(g != 1)
        def _():
            lsib(n, p).start()

    def collect(n):
        def one(i):
            pp = (p + 1 + i) % NP

            @pl.when(g > 0)
            def _():
                lgathered(n, pp).wait_recv()

            @pl.when(g != 1)
            def _():
                lsib(n, pp).start()

        loop(NP - 1, one)

    def prepare(n, dst):
        def one(i):
            pp = (p + i) % NP

            @pl.when(g > 0)
            def _():
                lsibbed(n, pp).wait_recv()

            prep(lb.at[n], dst, pp)

        loop(NP, one)

    lane = lax.broadcasted_iota(jnp.int32, (8, 128), 1)

    def pack(n, i):
        last = xf[n, 2 * i + 1, 1]
        for t in range(3):
            xc[n, g, i, t] = jnp.where(
                lane < RB, xf[n, 2 * i + t // 2, t % 2], pltpu.roll(last, RB - 32 * t, 1)
            )

    def plane(n, pp):
        v = xc.at[n, g]
        return rc(v, v, pgs.at[n, pp], pgr.at[n, p], pp * 2 + c, over(pp))

    def planed(n, pp):
        v = xc.at[n, pp * 2 + c]
        return rc(v, v, pgs.at[n, 0], pgr.at[n, pp], g, r)

    def sib(n, pp):
        v = xc.at[n, pp * 2 + c]
        return rc(v, v, sgs.at[n, pp], sgr.at[n, pp], g + 1 - 2 * c, r)

    def sibbed(n, pp):
        v = xc.at[n, pp * 2 + 1 - c]
        return rc(v, v, sgs.at[n, 0], sgr.at[n, pp], g, r)

    def spread(n):
        loop(8, lambda i: pack(n, i))
        sib(n, p).start()
        loop(NP - 1, lambda i: plane(n, (p + NP - 1 - i) % NP).start())

    def forward(n):
        def one(i):
            pp = (p + 1 + i) % NP
            planed(n, pp).wait_recv()
            sib(n, pp).start()

        loop(NP - 1, one)

    def lag_part(n, i):
        x = jnp.concatenate([xc[n, :, i, t].reshape(128, 128) for t in range(3)], axis=1)
        hi, lo = split(x)
        lhs = jnp.concatenate([hi, lo], axis=0).astype(BF16)
        o = jnp.dot(lhs, wl[i], preferred_element_type=F32)
        pa[...] += (o[0:128, 0:256] + o[128:256, 0:256]) + (o[0:128, 256:512] + o[128:256, 256:512])

    def lag_product(n):
        loop(NP, lambda i: sibbed(n, i).wait_recv())
        pa[...] = jnp.zeros_like(pa)
        loop(8, lambda i: lag_part(n, i))

    def turn(k):
        return (z // 2 + (1 - 2 * (k % 2)) * ((k + 1) // 2) + 8) % 8

    def qplane(i, pp):
        v = xc.at[2, g, i]
        return rc(v, v, qps.at[i, pp], qpr.at[i, p], pp * 2 + c, over(pp))

    def qplaned(i, pp):
        v = xc.at[2, pp * 2 + c, i]
        return rc(v, v, qps.at[i, 0], qpr.at[i, pp], g, r)

    def qsib(i, pp):
        v = xc.at[2, pp * 2 + c, i]
        return rc(v, v, qss.at[i, pp], qsr.at[i, pp], g + 1 - 2 * c, r)

    def qsibbed(i, pp):
        v = xc.at[2, pp * 2 + 1 - c, i]
        return rc(v, v, qss.at[i, 0], qsr.at[i, pp], g, r)

    def qspread(k):
        i = turn(k)
        pack(2, i)
        loop(NP - 1, lambda j: qplane(i, (p + NP - 1 - j) % NP).start())
        qsib(i, p).start()

    def qblock(zz, xx):
        @pl.when((zz != z) | (xx != xl))
        def _():
            block_from(xf.at[2], 1, zz, xx).wait_recv()

    def qgather(k):
        for j in range(4):
            qblock(2 * turn(k) + j // 2, j % 2)
        qspread(k)

    def qforward(k):
        i = turn(k)

        def one(j):
            pp = (p + 1 + j) % NP
            qplaned(i, pp).wait_recv()
            qsib(i, pp).start()

        loop(NP - 1, one)

    def qproduct(k):
        i = turn(k)
        loop(NP, lambda j: qsibbed(i, j).wait_recv())
        lag_part(2, i)

    def lag_rows(a):
        return pa[:, a * 128 : (a + 1) * 128].T[0:RB]

    def incoming(n):
        @pl.when(g < NG - 1)
        def _():
            rc(inc.at[n], inc.at[n], shs.at[n], shr.at[n], g, r).wait_recv()

        @pl.when(g == NG - 1)
        def _():
            inc[n] = jnp.zeros((RB, 128), F32)

    def advance(n):
        lag_product(n)
        incoming(n)
        first = hist[1] if n == 0 else accs[n - 1, 1]
        accs[n, 0] = first + lag_rows(0)
        accs[n, 1] = inc[n] + lag_rows(1)

        @pl.when(g > 0)
        def _():
            shift(n + 1, accs.at[n, 0]).start()

    prep_zero(wv)
    loc[0].wait()
    loop(8, lambda i: prep(invv, wv, i))
    for w in (w0, w1):
        prep_zero(w)
    loc[1].wait()

    def rwait(n):
        @pl.when(g != n // 2)
        def _():
            rscatter(n, g).wait_recv()

    rwait(0)
    send(xr.at[0], 0, rbuf[0], rx)

    @pl.when(g == 0)
    def _():
        loop(NG - 2, lambda i: lscatter(0, NG - 1 - i).wait_send())
        lscatter(0, 1).start()

    relay(0)
    now = product(xr.at[0], wv, 0, rx)
    send(xf.at[0], 1, now, xl)
    sent(xr.at[0], 0)

    @pl.when(g == 0)
    def _():
        loop(NG - 1, lambda i: lscatter(1, NG - 1 - i).start())

    collect(0)
    prepare(0, w0)
    rwait(1)
    now = rbuf[1] - product(xf.at[0], w0, 1, xl)
    send(xr.at[1], 0, now, rx)
    relay(1)
    sent(xf.at[0], 1)
    prep_lags()
    now = product(xr.at[1], wv, 0, rx)
    send(xf.at[1], 1, now, xl)
    spread(0)
    sent(xr.at[1], 0)
    collect(1)
    prepare(1, w1)
    rwait(2)
    late = rbuf[2] - product(xf.at[0], w1)
    now = late - product(xf.at[1], w0, 1, xl)
    send(xr.at[2], 0, now, rx)
    spread(1)
    sent(xf.at[1], 1)
    forward(0)
    advance(0)
    now = product(xr.at[2], wv, 0, rx)
    send_near(xf.at[2], 1, now, xl)
    sent(xr.at[2], 0)
    loop(3, qgather)
    forward(1)
    loop(5, lambda k: qgather(k + 3))
    sent(xf.at[2], 1)
    advance(1)
    @pl.when(g == 0)
    def _():
        for n in range(2):
            loop(NG - 1, lambda i, n=n: rscatter(n, 1 + i).wait_send())
            loop(NG - 1 if n else 1, lambda i, n=n: lscatter(n, 1 + i).wait_send())

    @pl.when(g == 1)
    def _():
        loop(NG - 1, lambda i: rscatter(2, (g + 1 + i) % NG).wait_send())

    for n in range(2):

        def lsent(i, n=n):
            pp = (p + 1 + i) % NP

            @pl.when(pp * 2 + c > 0)
            def _():
                lgather(n, pp).wait_send()

        loop(NP - 1, lsent)

        @pl.when(g != 1)
        def _(n=n):
            loop(NP, lambda i: lsib(n, i).wait_send())

        loop(NP - 1, lambda i, n=n: plane(n, (p + 1 + i) % NP).wait_send())
        loop(NP, lambda i, n=n: sib(n, i).wait_send())

        @pl.when(g > 0)
        def _(n=n):
            shift(n, accs.at[0, 0]).wait_send()

    def qplanesent(k):
        loop(NP - 1, lambda j: qplane(turn(k), (p + 1 + j) % NP).wait_send())

    def qsibsent(k):
        loop(NP, lambda j: qsib(turn(k), j).wait_send())

    pa[...] = jnp.zeros_like(pa)
    qforward(0)

    def last(k):
        qforward(k + 1)
        qproduct(k)
        qplanesent(k)
        qsibsent(k)

    loop(7, last)
    m = z // 2
    own = 2 * (z % 2) + xl

    @pl.when(own < 3)
    def _():
        cur_ref[...] = xc[2, :, m, own].reshape(128, 128).T[0:RB]

    @pl.when(own == 3)
    def _():
        for t in range(3):
            cur_ref[32 * t : 32 * t + 32] = xc[2, :, m, t].reshape(128, 128).T[RB:128]

    incoming(2)
    qproduct(7)
    fut_ref[0] = accs[1, 1] + lag_rows(0)
    fut_ref[1] = inc[2] + lag_rows(1)

    qsibsent(7)
    qplanesent(7)

    @pl.when(g > 0)
    def _():
        shift(2, accs.at[0, 0]).wait_send()


def body(lag_ops, inverse, history, loads):
    anyspec = pl.BlockSpec(memory_space=pl.ANY)
    vspec = pl.BlockSpec(memory_space=pltpu.VMEM)
    dma = pltpu.SemaphoreType.DMA
    scratch = [
        pltpu.VMEM((2, RB, U), F32),
        pltpu.VMEM((RB, U), F32),
        pltpu.VMEM((2, RB, 128), F32),
        pltpu.VMEM((3, RB, 128), F32),
        pltpu.VMEM((2, RB, U), F32),
        pltpu.VMEM((NZ, 256, 256), BF16),
        pltpu.VMEM((NZ, 256, 256), BF16),
        pltpu.VMEM((NZ, 256, 256), BF16),
        pltpu.VMEM((8, 384, 512), BF16),
        pltpu.VMEM((3, NZ, 2, 8, 128), F32),
        pltpu.VMEM((3, NZ, 2, 8, 128), F32),
        pltpu.VMEM((3, NG, 8, 3, 8, 128), F32),
        pltpu.VMEM((3, NG, 8, 128), F32),
        pltpu.VMEM((3, 8, 128), F32),
        pltpu.VMEM((3, RB, 128), F32),
        pltpu.VMEM((2, 2, RB, 128), F32),
        pltpu.VMEM((128, 256), F32),
        dma((5,)),
        dma((2, 2 * NZ)),
        dma((2, 2 * NZ)),
        dma((3, NG)),
        dma((3,)),
        dma((2, NG)),
        dma((2,)),
        dma((2, NP)),
        dma((2, NP)),
        dma((2, NP)),
        dma((2, NP)),
        dma((2, NP)),
        dma((2, NP)),
        dma((2, NP)),
        dma((2, NP)),
        dma((3,)),
        dma((3,)),
        dma((8, NP)),
        dma((8, NP)),
        dma((8, NP)),
        dma((8, NP)),
    ]
    return pl.pallas_call(
        kernel,
        out_shape=(
            pltpu.VMEM((RB, 128), F32),
            pltpu.VMEM((2, RB, 128), F32),
        ),
        in_specs=[anyspec] * 4,
        out_specs=(vspec, vspec),
        scratch_shapes=scratch,
        compiler_params=pltpu.CompilerParams(
            collective_id=0, has_side_effects=True, vmem_limit_bytes=60 * 2**20
        ),
    )(lag_ops, inverse, history, loads)


def solution(mesh):
    placed = (P("lag", "row", None), P("row", None), P("lag", "row", None), P(None, "row", None))
    return jax.shard_map(
        body,
        mesh=mesh,
        in_specs=placed,
        out_specs=(P("row", None), P("lag", "row", None)),
        check_vma=False,
    )
```

```python
import functools

import jax
import jax.numpy as jnp
from jax import lax
from jax.experimental import pallas as pl
from jax.experimental.pallas import tpu as pltpu
from jax.sharding import PartitionSpec as P

MESH = pl.DeviceIdType.MESH
F32 = jnp.float32
BF16 = jnp.bfloat16
NG = 16
NP = 8
NZ = 16
RB = 96
U = 3072
PC = U // NP
HR = RB // 2


def split(x):
    hi = x.astype(BF16).astype(F32)
    return hi, x - hi


def kernel(
    lag_h, inv_h, hist_h, loads_h, cur_ref, fut_ref,
    lagv, invv, hist, loads, lb, wv, w0, w1, wl, xr, xf, xc, tbuf, rbuf, inc, accs, pa,
    lsem, gs, gr, rss, rsr, lss, lsr, las, lar, lbs, lbr, pgs, pgr, sgs, sgr, shs, shr, qps, qpr, qss, qsr,
):
    g = lax.axis_index("lag")
    r = lax.axis_index("row")
    z, xl = r // 2, r % 2
    p, c = g // 2, g % 2
    xh = p % 2
    rx = (xl + xh) % 2

    def rc(src, dst, ss, rs, gg, rr):
        return pltpu.make_async_remote_copy(
            src_ref=src, dst_ref=dst, send_sem=ss, recv_sem=rs, device_id=(gg, rr), device_id_type=MESH
        )

    def loop(n, f):
        lax.fori_loop(0, n, lambda i, _: (f(i), 0)[1], 0)

    def over(pp):
        return z * 2 + (xl + xh + pp) % 2

    barrier = pltpu.get_barrier_semaphore()

    def greet(gg, rr):
        pl.semaphore_signal(barrier, inc=1, device_id=(gg, rr), device_id_type=MESH)

    loop(2 * NZ - 1, lambda i: greet(g, (r + 1 + i) % (2 * NZ)))
    loop(NG - 1, lambda i: greet((g + 1 + i) % NG, over((g + 1 + i) % NG // 2)))

    @pl.when((g > 0) & ((g - 1) // 2 % 2 != xh))
    def _():
        greet(g - 1, r)

    @pl.when((g < NG - 1) & ((g + 1) // 2 % 2 != xh))
    def _():
        greet(g + 1, r)

    extra = jnp.where((g > 0) & (g % 2 == 0), 1, 0) + jnp.where((g < NG - 1) & (g % 2 == 1), 1, 0)

    loc = [
        pltpu.make_async_copy(inv_h, invv, lsem.at[0]),
        pltpu.make_async_copy(lag_h, lagv, lsem.at[1]),
        pltpu.make_async_copy(hist_h, hist, lsem.at[2]),
        pltpu.make_async_copy(loads_h, loads, lsem.at[3]),
    ]
    for cp in (loc[3], loc[2], loc[0], loc[1]):
        cp.start()
    root = pltpu.make_async_copy(lag_h, lb, lsem.at[4])

    @pl.when(g == 0)
    def _():
        root.start()

    loc[3].wait()
    loc[2].wait()

    def turned(n, h):
        d = loads[n] - hist[h]
        return jnp.concatenate([d, jnp.zeros((128 - RB, 128), F32)], axis=0).T.reshape(NG, 8, 128)

    @pl.when(g == 0)
    def _():
        t0 = turned(0, 0)
        tbuf[0] = t0
        rbuf[0] = t0[0]
        t1 = turned(1, 1)
        tbuf[1] = t1
        rbuf[1] = t1[0]
        root.wait()

    @pl.when(g == 1)
    def _():
        t2 = turned(2, 0)
        tbuf[2] = t2
        rbuf[2] = t2[1]

    pl.semaphore_wait(barrier, 2 * NZ - 1 + NG - 1 + extra)

    def rscatter(n, gg):
        return rc(tbuf.at[n, gg], rbuf.at[n], rss.at[n, gg], rsr.at[n], gg, over(gg // 2))

    def piece(n, cc, pp):
        return lb.at[n, pl.ds(pl.multiple_of(cc * HR, 8), HR), pl.ds(pl.multiple_of(pp * PC, 128), PC)]

    def lscatter(n, gg):
        v = piece(n, gg % 2, gg // 2)
        return rc(v, v, lss.at[n, gg], lsr.at[n], gg, over(gg // 2))

    @pl.when(g == 0)
    def _():
        loop(NG - 1, lambda i: rscatter(0, NG - 1 - i).start())
        loop(NG - 2, lambda i: lscatter(0, NG - 1 - i).start())
        loop(NG - 1, lambda i: rscatter(1, NG - 1 - i).start())

    @pl.when(g == 1)
    def _():
        loop(NG - 1, lambda i: rscatter(2, (g + 1 + i) % NG).start())

    def shift(n, src):
        return rc(src, inc.at[n], shs.at[n], shr.at[n], g - 1, r)

    @pl.when(g > 0)
    def _():
        shift(0, hist.at[0]).start()

    def prep_zero(dst):
        for f in range(2):
            dst[:, f * 128 + RB : (f + 1) * 128, :] = jnp.zeros((NZ, 128 - RB, 256), BF16)

    def turned_parts(blk):
        hi, lo = split(jnp.concatenate([blk, jnp.zeros((128 - RB, 384), F32)], axis=0).T)
        return hi.astype(BF16), lo.astype(BF16)

    def prep(src, dst, i):
        hi, lo = turned_parts(src[:, pl.ds(pl.multiple_of(i * 384, 128), 384)])
        for j in range(4):
            rows = slice((j % 2) * 128, (j % 2) * 128 + RB)
            dst[2 * i + j // 2, rows, 0:128] = hi[j * RB : (j + 1) * RB]
            dst[2 * i + j // 2, rows, 128:256] = lo[j * RB : (j + 1) * RB]

    def prep_lags():
        def some(i):
            for a in range(2):
                hi, lo = turned_parts(lagv[a, :, pl.ds(pl.multiple_of(i * 384, 128), 384)])
                for part, n in ((hi, a * 128), (lo, 256 + a * 128)):
                    for t in range(3):
                        wl[i, t * 128 : t * 128 + RB, n : n + 128] = part[t * RB : (t + 1) * RB]
                        wl[i, t * 128 + RB : (t + 1) * 128, n : n + 128] = part[288 + 32 * t : 320 + 32 * t]

        loop(8, some)

    def at_turn(k):
        return (z + (2 * (k % 2) - 1) * (8 - (k + 1) // 2) + NZ) % NZ

    def block_to(xb, par, k, f, own):
        zz = at_turn(k)
        xx = (xl + 1 - f) % 2
        v = xb.at[z, own]
        return rc(v, v, gs.at[par, 2 * k + f], gr.at[par, z * 2 + own], g, zz * 2 + xx)

    def block_from(xb, par, zz, xx):
        v = xb.at[zz, xx]
        return rc(v, v, gs.at[par, 0], gr.at[par, zz * 2 + xx], g, r)

    def send(xb, par, block, own):
        xb[z, own] = block

        def one(i):
            block_to(xb, par, i // 2, i % 2, own).start()

        loop(2 * NZ - 1, one)

    def send_near(xb, par, block, own):
        xb[z, own] = block
        block_to(xb, par, 0, 0, own).start()
        block_to(xb, par, 0, 1, own).start()

        def one(i):
            j = 2 * NZ - 2 - i
            block_to(xb, par, j // 2, j % 2, own).start()

        loop(2 * NZ - 3, one)

    def sent(xb, par):
        loop(2 * NZ - 1, lambda i: block_to(xb, par, i // 2, i % 2, xl).wait_send())

    def arrived(xb, par, own, k):
        zz = at_turn(k)
        block_from(xb, par, zz, 1 - own).wait_recv()
        if k < NZ - 1:
            block_from(xb, par, zz, own).wait_recv()

    def product(xb, w, par=None, own=None):
        acc = [jnp.zeros((16, 256), F32), jnp.zeros((16, 256), F32)]
        for batch in ((15, 14, 13, 12, 11, 10, 9), (8, 7, 6, 5), (4, 3), (2, 1, 0)):
            if par is not None:
                for k in batch:
                    arrived(xb, par, own, k)
            for k in batch:
                zz = at_turn(k)
                x = jnp.concatenate([xb[zz, 0], xb[zz, 1]], axis=1)
                hi, lo = split(x)
                lhs = jnp.concatenate([hi, lo], axis=0).astype(BF16)
                acc[k % 2] += jnp.dot(lhs, w[zz], preferred_element_type=F32)
        acc = acc[0] + acc[1]
        return (acc[0:8, 0:128] + acc[8:16, 0:128]) + (acc[0:8, 128:256] + acc[8:16, 128:256])

    def lgather(n, pp):
        v = piece(n, c, p)
        return rc(v, v, las.at[n, pp], lar.at[n, p], pp * 2 + c, over(pp))

    def lgathered(n, pp):
        v = piece(n, c, pp)
        return rc(v, v, las.at[n, 0], lar.at[n, pp], g, r)

    def lsib(n, pp):
        v = piece(n, c, pp)
        return rc(v, v, lbs.at[n, pp], lbr.at[n, pp], g + 1 - 2 * c, r)

    def lsibbed(n, pp):
        v = piece(n, 1 - c, pp)
        return rc(v, v, lbs.at[n, 0], lbr.at[n, pp], g, r)

    def relay(n):
        @pl.when(g > 0)
        def _():
            lscatter(n, g).wait_recv()

        def one(i):
            pp = (p + 1 + i) % NP

            @pl.when(pp * 2 + c > 0)
            def _():
                lgather(n, pp).start()

        loop(NP - 1, one)

        @pl.when(g != 1)
        def _():
            lsib(n, p).start()

    def collect(n):
        def one(i):
            pp = (p + 1 + i) % NP

            @pl.when(g > 0)
            def _():
                lgathered(n, pp).wait_recv()

            @pl.when(g != 1)
            def _():
                lsib(n, pp).start()

        loop(NP - 1, one)

    def prepare(n, dst):
        def one(i):
            pp = (p + i) % NP

            @pl.when(g > 0)
            def _():
                lsibbed(n, pp).wait_recv()

            prep(lb.at[n], dst, pp)

        loop(NP, one)

    lane = lax.broadcasted_iota(jnp.int32, (8, 128), 1)

    def pack(n, i):
        last = xf[n, 2 * i + 1, 1]
        for t in range(3):
            xc[n, g, i, t] = jnp.where(
                lane < RB, xf[n, 2 * i + t // 2, t % 2], pltpu.roll(last, RB - 32 * t, 1)
            )

    far_first = ((2, 1), (2, 0), (1, 1), (3, 1), (1, 0), (3, 0), (0, 1))

    def peer(dy, dx):
        return (p // 2 + dy) % 4 * 2 + (xh + dx) % 2

    def plane(n, pp):
        v = xc.at[n, g]
        return rc(v, v, pgs.at[n, pp], pgr.at[n, p], pp * 2 + c, over(pp))

    def planed(n, pp):
        v = xc.at[n, pp * 2 + c]
        return rc(v, v, pgs.at[n, 0], pgr.at[n, pp], g, r)

    def sib(n, pp):
        v = xc.at[n, pp * 2 + c]
        return rc(v, v, sgs.at[n, pp], sgr.at[n, pp], g + 1 - 2 * c, r)

    def sibbed(n, pp):
        v = xc.at[n, pp * 2 + 1 - c]
        return rc(v, v, sgs.at[n, 0], sgr.at[n, pp], g, r)

    def spread(n):
        loop(8, lambda i: pack(n, i))
        sib(n, p).start()
        for d in far_first:
            plane(n, peer(*d)).start()

    def forward(n):
        def one(i):
            pp = (p + 1 + i) % NP
            planed(n, pp).wait_recv()
            sib(n, pp).start()

        loop(NP - 1, one)

    def lag_part(n, i):
        x = jnp.concatenate([xc[n, :, i, t].reshape(128, 128) for t in range(3)], axis=1)
        hi, lo = split(x)
        lhs = jnp.concatenate([hi, lo], axis=0).astype(BF16)
        o = jnp.dot(lhs, wl[i], preferred_element_type=F32)
        pa[...] += (o[0:128, 0:256] + o[128:256, 0:256]) + (o[0:128, 256:512] + o[128:256, 256:512])

    def lag_product(n):
        loop(NP, lambda i: sibbed(n, i).wait_recv())
        pa[...] = jnp.zeros_like(pa)
        loop(8, lambda i: lag_part(n, i))

    def turn(k):
        return (z // 2 + (1 - 2 * (k % 2)) * ((k + 1) // 2) + 8) % 8

    def qplane(i, pp):
        v = xc.at[2, g, i]
        return rc(v, v, qps.at[i, pp], qpr.at[i, p], pp * 2 + c, over(pp))

    def qplaned(i, pp):
        v = xc.at[2, pp * 2 + c, i]
        return rc(v, v, qps.at[i, 0], qpr.at[i, pp], g, r)

    def qsib(i, pp):
        v = xc.at[2, pp * 2 + c, i]
        return rc(v, v, qss.at[i, pp], qsr.at[i, pp], g + 1 - 2 * c, r)

    def qsibbed(i, pp):
        v = xc.at[2, pp * 2 + 1 - c, i]
        return rc(v, v, qss.at[i, 0], qsr.at[i, pp], g, r)

    def qspread(k):
        i = turn(k)
        pack(2, i)
        for d in far_first:
            qplane(i, peer(*d)).start()
        qsib(i, p).start()

    def qblock(zz, xx):
        @pl.when((zz != z) | (xx != xl))
        def _():
            block_from(xf.at[2], 1, zz, xx).wait_recv()

    def qgather(k):
        for j in range(4):
            qblock(2 * turn(k) + j // 2, j % 2)
        qspread(k)

    def qforward(k):
        i = turn(k)

        def one(j):
            pp = (p + 1 + j) % NP
            qplaned(i, pp).wait_recv()
            qsib(i, pp).start()

        loop(NP - 1, one)

    def qproduct(k):
        i = turn(k)
        loop(NP, lambda j: qsibbed(i, j).wait_recv())
        lag_part(2, i)

    def lag_rows(a):
        return pa[:, a * 128 : (a + 1) * 128].T[0:RB]

    def incoming(n):
        @pl.when(g < NG - 1)
        def _():
            rc(inc.at[n], inc.at[n], shs.at[n], shr.at[n], g, r).wait_recv()

        @pl.when(g == NG - 1)
        def _():
            inc[n] = jnp.zeros((RB, 128), F32)

    def advance(n):
        lag_product(n)
        incoming(n)
        first = hist[1] if n == 0 else accs[n - 1, 1]
        accs[n, 0] = first + lag_rows(0)
        accs[n, 1] = inc[n] + lag_rows(1)

        @pl.when(g > 0)
        def _():
            shift(n + 1, accs.at[n, 0]).start()

    prep_zero(wv)
    loc[0].wait()
    loop(8, lambda i: prep(invv, wv, i))
    for w in (w0, w1):
        prep_zero(w)
    loc[1].wait()

    def rwait(n):
        @pl.when(g != n // 2)
        def _():
            rscatter(n, g).wait_recv()

    rwait(0)
    send(xr.at[0], 0, rbuf[0], rx)

    @pl.when(g == 0)
    def _():
        loop(NG - 2, lambda i: lscatter(0, NG - 1 - i).wait_send())
        lscatter(0, 1).start()

    relay(0)
    now = product(xr.at[0], wv, 0, rx)
    send(xf.at[0], 1, now, xl)
    sent(xr.at[0], 0)

    @pl.when(g == 0)
    def _():
        loop(NG - 1, lambda i: lscatter(1, NG - 1 - i).start())

    collect(0)
    prepare(0, w0)
    rwait(1)
    now = rbuf[1] - product(xf.at[0], w0, 1, xl)
    send(xr.at[1], 0, now, rx)
    relay(1)
    sent(xf.at[0], 1)
    prep_lags()
    now = product(xr.at[1], wv, 0, rx)
    send(xf.at[1], 1, now, xl)
    spread(0)
    sent(xr.at[1], 0)
    collect(1)
    prepare(1, w1)
    rwait(2)
    late = rbuf[2] - product(xf.at[0], w1)
    now = late - product(xf.at[1], w0, 1, xl)
    send(xr.at[2], 0, now, rx)
    spread(1)
    sent(xf.at[1], 1)
    forward(0)
    advance(0)
    now = product(xr.at[2], wv, 0, rx)
    send_near(xf.at[2], 1, now, xl)
    sent(xr.at[2], 0)
    loop(3, qgather)
    forward(1)
    loop(5, lambda k: qgather(k + 3))
    sent(xf.at[2], 1)
    advance(1)
    @pl.when(g == 0)
    def _():
        for n in range(2):
            loop(NG - 1, lambda i, n=n: rscatter(n, 1 + i).wait_send())
            loop(NG - 1 if n else 1, lambda i, n=n: lscatter(n, 1 + i).wait_send())

    @pl.when(g == 1)
    def _():
        loop(NG - 1, lambda i: rscatter(2, (g + 1 + i) % NG).wait_send())

    for n in range(2):

        def lsent(i, n=n):
            pp = (p + 1 + i) % NP

            @pl.when(pp * 2 + c > 0)
            def _():
                lgather(n, pp).wait_send()

        loop(NP - 1, lsent)

        @pl.when(g != 1)
        def _(n=n):
            loop(NP, lambda i: lsib(n, i).wait_send())

        loop(NP - 1, lambda i, n=n: plane(n, (p + 1 + i) % NP).wait_send())
        loop(NP, lambda i, n=n: sib(n, i).wait_send())

        @pl.when(g > 0)
        def _(n=n):
            shift(n, accs.at[0, 0]).wait_send()

    def qplanesent(k):
        loop(NP - 1, lambda j: qplane(turn(k), (p + 1 + j) % NP).wait_send())

    def qsibsent(k):
        loop(NP, lambda j: qsib(turn(k), j).wait_send())

    pa[...] = jnp.zeros_like(pa)
    qforward(0)

    def last(k):
        qforward(k + 1)
        qproduct(k)
        qplanesent(k)
        qsibsent(k)

    last(0)
    m = z // 2
    own = 2 * (z % 2) + xl

    @pl.when(own < 3)
    def _():
        cur_ref[...] = xc[2, :, m, own].reshape(128, 128).T[0:RB]

    @pl.when(own == 3)
    def _():
        for t in range(3):
            cur_ref[32 * t : 32 * t + 32] = xc[2, :, m, t].reshape(128, 128).T[RB:128]

    loop(6, lambda k: last(k + 1))
    incoming(2)
    qplanesent(7)

    @pl.when(g > 0)
    def _():
        shift(2, accs.at[0, 0]).wait_send()

    qproduct(7)
    fut_ref[0] = accs[1, 1] + lag_rows(0)
    fut_ref[1] = inc[2] + lag_rows(1)

    qsibsent(7)


def body(lag_ops, inverse, history, loads):
    anyspec = pl.BlockSpec(memory_space=pl.ANY)
    vspec = pl.BlockSpec(memory_space=pltpu.VMEM)
    dma = pltpu.SemaphoreType.DMA
    scratch = [
        pltpu.VMEM((2, RB, U), F32),
        pltpu.VMEM((RB, U), F32),
        pltpu.VMEM((2, RB, 128), F32),
        pltpu.VMEM((3, RB, 128), F32),
        pltpu.VMEM((2, RB, U), F32),
        pltpu.VMEM((NZ, 256, 256), BF16),
        pltpu.VMEM((NZ, 256, 256), BF16),
        pltpu.VMEM((NZ, 256, 256), BF16),
        pltpu.VMEM((8, 384, 512), BF16),
        pltpu.VMEM((3, NZ, 2, 8, 128), F32),
        pltpu.VMEM((3, NZ, 2, 8, 128), F32),
        pltpu.VMEM((3, NG, 8, 3, 8, 128), F32),
        pltpu.VMEM((3, NG, 8, 128), F32),
        pltpu.VMEM((3, 8, 128), F32),
        pltpu.VMEM((3, RB, 128), F32),
        pltpu.VMEM((2, 2, RB, 128), F32),
        pltpu.VMEM((128, 256), F32),
        dma((5,)),
        dma((2, 2 * NZ)),
        dma((2, 2 * NZ)),
        dma((3, NG)),
        dma((3,)),
        dma((2, NG)),
        dma((2,)),
        dma((2, NP)),
        dma((2, NP)),
        dma((2, NP)),
        dma((2, NP)),
        dma((2, NP)),
        dma((2, NP)),
        dma((2, NP)),
        dma((2, NP)),
        dma((3,)),
        dma((3,)),
        dma((8, NP)),
        dma((8, NP)),
        dma((8, NP)),
        dma((8, NP)),
    ]
    return pl.pallas_call(
        kernel,
        out_shape=(
            pltpu.VMEM((RB, 128), F32),
            pltpu.VMEM((2, RB, 128), F32),
        ),
        in_specs=[anyspec] * 4,
        out_specs=(vspec, vspec),
        scratch_shapes=scratch,
        compiler_params=pltpu.CompilerParams(
            collective_id=0, has_side_effects=True, vmem_limit_bytes=60 * 2**20
        ),
    )(lag_ops, inverse, history, loads)


def solution(mesh):
    placed = (P("lag", "row", None), P("row", None), P("lag", "row", None), P(None, "row", None))
    return jax.shard_map(
        body,
        mesh=mesh,
        in_specs=placed,
        out_specs=(P("row", None), P("lag", "row", None)),
        check_vma=False,
    )
```
